512 devices in a mesh: dp: 16 (over y, core), label: 32 (over z, x).
Axes of the slice: x: 4, y: 8, z: 8, core: 2. Of those that a mesh axis runs over, the one named last changes fastest.
Arguments:
- feats: bfloat16 [8192, 1024], P('dp'), may hold values from -2 to 2
- weights: bfloat16 [2048, 256, 1024], P(('dp', 'label')), may hold values from -5 to 5
- shortlist: int32 [64, 256], replicated, may hold values from 0 to 2047, as said below
- slot_of: int32 [2048], replicated, may hold values from 0 to 2047, as said below
- positives: int32 [8192, 8], P('dp'), may hold values from 0 to 524287, as said below
Outputs:
- loss: float32 [8192], P('dp')
- grad_feats: bfloat16 [8192, 1024], P('dp', 'label')
The draws below stay inside these ranges and needn't reach their ends.
Inputs may be any that keep to these rules, and one draw needn't show every extreme that they name: `slot_of`: A permutation of the cluster ids: the slot of each cluster. For each index d of dp, its blocks d * 4 to d * 4 + 3: the first 2 of them together shortlist one cluster stored on each device (the device of slot s being s // 4 in the order of the weights' placement), each once, and the last 2 shortlist the same clusters, each once; so every such cluster is shortlisted by exactly two blocks of d. `positives`: an instance's 8 labels are different, and each lies in a cluster that the instance's block shortlists.
All inputs are finite; a program needn't handle non-finite values.
Results may differ from the reference program's by a relative error of at most 0.0034.
Values may be sent and summed in bfloat16 or wider, within the bound.
A program may use at most 64 MiB of HBM per device.

```python
import math
import jax
import jax.numpy as jnp
from jax import lax

D = 1024
CS = 256
BLK = 128
POS = 8
CL_DEV = 4
NB = 4
KB = 256
INST = 8192
NBT = 64
NCL = 2048
N_DP = 16
N_LABEL = 32


def cluster_rows(key, slot):
    sub_key = jax.random.fold_in(jax.random.fold_in(key, 13), slot)
    values = jnp.clip(jax.random.normal(sub_key, (CS, D), jnp.float32), -5.0, 5.0)
    return values


def slot_table(key):
    return jax.random.permutation(jax.random.fold_in(key, 11), NCL).astype(jnp.int32)


def shortlist_table(key):
    slot_of = slot_table(key)
    cluster_at = jnp.zeros((NCL,), jnp.int32).at[slot_of].set(jnp.arange(NCL, dtype=jnp.int32))
    dev_total = N_DP * N_LABEL
    local_key, first_key, second_key = jax.random.split(jax.random.fold_in(key, 12), 3)
    local_ids = jax.random.randint(local_key, (N_DP, dev_total), 0, CL_DEV)
    chosen = cluster_at[jnp.arange(dev_total, dtype=jnp.int32)[None, :] * CL_DEV + local_ids]
    first_order = jax.vmap(lambda sub_key: jax.random.permutation(sub_key, dev_total))(jax.random.split(first_key, N_DP))
    second_order = jax.vmap(lambda sub_key: jax.random.permutation(sub_key, dev_total))(jax.random.split(second_key, N_DP))
    low_half = jnp.take_along_axis(chosen, first_order, axis=1).reshape(N_DP, NB // 2, KB)
    high_half = jnp.take_along_axis(chosen, second_order, axis=1).reshape(N_DP, NB // 2, KB)
    return jnp.concatenate([low_half, high_half], axis=1).reshape(NBT, KB).astype(jnp.int32)


def draw_slot_of(key, part):
    return slot_table(key)


def draw_shortlist(key, part):
    return shortlist_table(key)


def draw_weights(key, part):
    values = jax.vmap(lambda slot: cluster_rows(key, slot))(jnp.arange(NCL, dtype=jnp.int32))
    return values.astype(jnp.bfloat16)


def draw_positives(key, part):
    shortlist = shortlist_table(key)
    pick_key, offset_key = jax.random.split(jax.random.fold_in(key, 14))
    picks = jax.random.randint(pick_key, (INST, POS), 0, KB)
    stride = CS // POS
    offsets = jnp.arange(POS, dtype=jnp.int32)[None, :] * stride + jax.random.randint(offset_key, (INST, POS), 0, stride)
    block_ids = jnp.arange(INST, dtype=jnp.int32) // BLK
    clusters = shortlist[block_ids[:, None], picks]
    return (clusters * CS + offsets).astype(jnp.int32)


def draw_feats(key, part):
    base_key = jax.random.fold_in(key, 15)
    value_key = jax.random.fold_in(base_key, 1)
    spread = 3.0 / math.sqrt(D)
    values = jnp.clip(jax.random.normal(value_key, (INST, D), jnp.float32), -6.0, 6.0) * spread
    return values.astype(jnp.bfloat16)


def setup_inputs(seed: int = 0) -> dict:
    keys = jax.random.split(jax.random.key(seed), 6)
    return {
        "feats": draw_feats(jax.random.fold_in(keys[5], 71), 0),
        "weights": draw_weights(jax.random.fold_in(keys[5], 71), 0),
        "shortlist": draw_shortlist(jax.random.fold_in(keys[5], 71), 0),
        "slot_of": draw_slot_of(jax.random.fold_in(keys[5], 71), 0),
        "positives": draw_positives(jax.random.fold_in(keys[5], 71), 0),
    }


def block_terms(feat_block, clusters, pos_block, weights, slot_of):
    slots = slot_of[clusters]
    table = weights[slots].reshape(KB * CS, D)
    logits = jnp.dot(feat_block, table.T, preferred_element_type=jnp.float32)
    highest = jnp.max(logits, axis=1)
    total = jnp.sum(jnp.exp(logits - highest[:, None]), axis=1)
    log_sum = highest + jnp.log(total)
    pos_cluster = pos_block // CS
    pos_offset = pos_block % CS
    cluster_match = (pos_cluster[:, :, None] == clusters[None, None, :]).astype(jnp.float32)
    offset_hot = (pos_offset[:, :, None] == jnp.arange(CS, dtype=jnp.int32)[None, None, :]).astype(jnp.float32)
    target = jnp.einsum("ipk,ipo->iko", cluster_match, offset_hot).reshape(BLK, KB * CS)
    pos_total = jnp.sum(target * logits, axis=1)
    loss_rows = log_sum - pos_total / POS
    dlogit = (jnp.exp(logits - log_sum[:, None]) - target / POS).astype(jnp.bfloat16)
    grads = jnp.dot(dlogit, table, preferred_element_type=jnp.float32).astype(jnp.bfloat16)
    return loss_rows, grads


def reference(feats, weights, shortlist, slot_of, positives):
    blocks = feats.shape[0] // BLK

    def one_block(items):
        feat_block, clusters, pos_block = items
        return block_terms(feat_block, clusters, pos_block, weights, slot_of)

    loss_rows, grads = lax.map(one_block, (feats.reshape(blocks, BLK, D), shortlist, positives.reshape(blocks, BLK, POS)))
    return loss_rows.reshape(-1), grads.reshape(-1, D)
```

```python
import functools
import itertools

import jax
import jax.numpy as jnp
from jax import lax
from jax.experimental import pallas as pl
from jax.experimental.pallas import tpu as pltpu
from jax.sharding import PartitionSpec as P

BLK = 128
CORES = 2
X_CHIPS = 4
VMEM_LIMIT = 56 * 1024 * 1024
NEG_FILL = -1e30
MESH = pl.DeviceIdType.MESH


class Place:
    def __init__(self, y_count, z_count, x_count):
        dp, lab = lax.axis_index("dp"), lax.axis_index("label")
        self.dp, self.lab = dp, lab
        self.y, self.core = dp // CORES, dp % CORES
        self.z, self.x = lab // x_count, lab % x_count
        self.count = {"y": y_count, "z": z_count, "x": x_count}
        self.pos = {"y": self.y, "z": self.z, "x": self.x}

    def at(self, axis, offset):
        n = self.count[axis]
        return lax.rem(self.pos[axis] + (offset % n), n)

    def device(self, axis, offset):
        p = self.at(axis, offset)
        if axis == "y":
            return (p * CORES + self.core, self.lab)
        if axis == "z":
            return (self.dp, p * self.count["x"] + self.x)
        return (self.dp, self.z * self.count["x"] + p)

    def sibling(self):
        return (self.y * CORES + (1 - self.core), self.lab)


def greet(devices):
    barrier = pltpu.get_barrier_semaphore()
    for device in devices:
        pl.semaphore_signal(barrier, inc=1, device_id=device, device_id_type=MESH)
    pl.semaphore_wait(barrier, len(devices))


class Sender:
    def __init__(self, send_sem, recv_sem):
        self.send_sem, self.recv_sem = send_sem, recv_sem
        self.ids = itertools.count()
        self.sent = []

    def start(self, src, dst, device):
        i = next(self.ids)
        copy = pltpu.make_async_remote_copy(
            src_ref=src,
            dst_ref=dst,
            send_sem=self.send_sem.at[i],
            recv_sem=self.recv_sem.at[i],
            device_id=device,
            device_id_type=MESH,
        )
        copy.start()
        self.sent.append(copy)
        return copy

    def drain(self):
        for copy in self.sent:
            copy.wait_send()


def reach(n, sign, half):
    return n // 2 if (sign > 0) == (half == 0) else n // 2 - 1


class Spread:
    def __init__(self, place, axis, half, source, target, sender, arrived=None):
        self.place, self.axis, self.half = place, axis, half
        self.source, self.target, self.sender = source, target, sender
        self.arrived = arrived
        self.step = 0
        self.copies = {}

    def advance(self):
        n = self.place.count[self.axis]
        k = self.step
        born = []
        for sign in (1, -1):
            limit = reach(n, sign, self.half)
            origin = self.place.at(self.axis, -sign * k)
            if 1 <= k <= limit:
                self.copies[sign, k].wait_recv()
                if self.arrived is not None:
                    born += self.arrived(origin)
            if k + 1 <= limit:
                src = self.source() if k == 0 else self.target(origin)
                self.copies[sign, k + 1] = self.sender.start(
                    src, self.target(origin), self.place.device(self.axis, sign)
                )
        self.step += 1
        return born, self.step > n // 2


def run_all(tasks):
    while tasks:
        left, born_now = [], []
        for task in tasks:
            born, done = task.advance()
            born_now += born
            if not done:
                left.append(task)
        tasks = left + born_now


def gather_kernel(sizes, feats, pos, rows, f_all, p_all, w_sib, local_sem, send_sem, recv_sem):
    y_count, z_count, x_count = sizes
    place = Place(*sizes)
    inst, width = feats.shape
    a_total, b_total = inst // 2, inst // 4
    a_part, b_part = a_total // x_count, b_total // z_count
    c_total = inst - a_total - b_total
    greet(
        [place.device(axis, offset) for axis in "yxz" for offset in (1, -1)] + [place.sibling()]
    )
    sender = Sender(send_sem, recv_sem)
    mine = place.y

    def piece(start, count):
        start = pl.multiple_of(start, 16)
        return (
            lambda: feats.at[pl.ds(start, count)],
            lambda origin: f_all.at[origin, pl.ds(start, count)],
        )

    tasks = []
    a_half = a_part // 2
    for half in (0, 1):
        source, target = piece(c_total + place.x * a_part + half * a_half, a_half)

        def a_arrived(origin, half=half, target=target):
            def moved(o, origin=origin, half=half):
                start = pl.multiple_of(c_total + o * a_part + half * a_half, 16)
                return f_all.at[origin, pl.ds(start, a_half)]

            return [Spread(place, "x", half, lambda: target(origin), moved, sender)]

        tasks.append(Spread(place, "y", half, source, target, sender, a_arrived))
    source, target = piece(c_total + a_total + place.z * b_part, b_part)
    order = itertools.count()

    def b_arrived(origin, target=target):
        def moved(o, origin=origin):
            start = pl.multiple_of(c_total + a_total + o * b_part, 16)
            return f_all.at[origin, pl.ds(start, b_part)]

        return [Spread(place, "z", next(order) % 2, lambda: target(origin), moved, sender)]

    tasks.append(Spread(place, "y", 0, source, target, sender, b_arrived))
    tasks.append(Spread(place, "y", 1, lambda: pos, lambda origin: p_all.at[origin], sender))
    for half in (0, 1):
        source, target = piece(half * (c_total // 2), c_total // 2)
        tasks.append(Spread(place, "y", half, source, target, sender))

    swap = sender.start(rows, w_sib, place.sibling())
    keep_f = pltpu.make_async_copy(feats, f_all.at[mine], local_sem.at[0])
    keep_p = pltpu.make_async_copy(pos, p_all.at[mine], local_sem.at[1])
    keep_f.start()
    keep_p.start()
    run_all(tasks)
    swap.wait_recv()
    keep_f.wait()
    keep_p.wait()
    sender.drain()


def gather(sizes, feats, pos, rows):
    y_count, z_count, x_count = sizes
    copies = 6 * (y_count - 1) + (y_count - 1) * (2 * (x_count - 1) + z_count - 1) + 1
    return pl.pallas_call(
        functools.partial(gather_kernel, sizes),
        out_shape=(
            jax.ShapeDtypeStruct((y_count,) + feats.shape, feats.dtype),
            jax.ShapeDtypeStruct((y_count,) + pos.shape, pos.dtype),
            jax.ShapeDtypeStruct(rows.shape, rows.dtype),
        ),
        in_specs=[pl.BlockSpec(memory_space=pl.ANY)] * 3,
        out_specs=[pl.BlockSpec(memory_space=pl.ANY)] * 3,
        scratch_shapes=[
            pltpu.SemaphoreType.DMA((2,)),
            pltpu.SemaphoreType.DMA((copies,)),
            pltpu.SemaphoreType.DMA((copies,)),
        ],
        compiler_params=pltpu.CompilerParams(
            collective_id=0, has_side_effects=True, vmem_limit_bytes=VMEM_LIMIT
        ),
    )(feats, pos, rows)


def target_of(pos_ref, cluster, shape):
    size = shape[0]
    label = cluster * size + lax.broadcasted_iota(jnp.int32, shape, 0)
    hit = pos_ref[0, 0:1, :] == label
    for p in range(1, pos_ref.shape[1]):
        hit = hit | (pos_ref[0, p : p + 1, :] == label)
    return hit


def logits_kernel(pick, cluster, f_ref, own_ref, sib_ref, mask_ref, pos_ref, kept_ref, stat_ref):
    d = pl.program_id(0)
    feats = f_ref[0]
    highs, sums, hits = [], [], []
    for s, rows_ref in enumerate((own_ref, sib_ref)):
        logits = lax.dot_general(
            rows_ref[0], feats, (((1,), (1,)), ((), ())), preferred_element_type=jnp.float32
        )
        kept_ref[0, s] = logits
        valid = jnp.where(mask_ref[0, s : s + 1, :] > 0, logits, NEG_FILL)
        high = jnp.max(valid, axis=0, keepdims=True)
        highs.append(high)
        sums.append(jnp.sum(jnp.exp(valid - high), axis=0, keepdims=True))
        hit = target_of(pos_ref, cluster[d, s], logits.shape)
        hits.append(jnp.sum(jnp.where(hit, logits, 0.0), axis=0, keepdims=True))
    high = jnp.maximum(highs[0], highs[1])
    total = sums[0] * jnp.exp(highs[0] - high) + sums[1] * jnp.exp(highs[1] - high)
    stat_ref[0] = jnp.zeros_like(stat_ref[0])
    stat_ref[0, 0:1, :] = high
    stat_ref[0, 1:2, :] = total
    stat_ref[0, 2:3, :] = hits[0] + hits[1]


def grads_kernel(pick, cluster, own_ref, sib_ref, mask_ref, pos_ref, kept_ref, lse_ref, gx_ref, gz_ref):
    d = pl.program_id(0)
    pos_count = pos_ref.shape[1]
    shares = None
    lse = lse_ref[0, 0:1, :]
    for s, rows_ref in enumerate((own_ref, sib_ref)):
        logits = kept_ref[0, s]
        prob = jnp.where(mask_ref[0, s : s + 1, :] > 0, jnp.exp(logits - lse), 0.0)
        hit = target_of(pos_ref, cluster[d, s], logits.shape)
        dlogit = (prob - jnp.where(hit, 1.0 / pos_count, 0.0)).astype(jnp.bfloat16)
        term = lax.dot_general(
            rows_ref[0], dlogit, (((0,), (0,)), ((), ())), preferred_element_type=jnp.float32
        )
        shares = term if shares is None else shares + term
    half = shares.shape[1] // 2
    gx_ref[0] = shares[:, :half].astype(jnp.bfloat16)
    gz_ref[0] = shares[:, half:].astype(jnp.bfloat16)


def block(shape):
    return pl.BlockSpec((1,) + shape, lambda d, pick, cluster: (d,) + (0,) * len(shape))


def picked(s, rows):
    return pl.BlockSpec((1,) + rows.shape[1:], lambda d, pick, cluster: (pick[d, s], 0, 0))


def first_pass(pick, cluster, f_all, own, sib, mask, pos):
    y_count, inst, width = f_all.shape
    size = own.shape[1]
    return pl.pallas_call(
        logits_kernel,
        grid_spec=pltpu.PrefetchScalarGridSpec(
            num_scalar_prefetch=2,
            grid=(y_count,),
            in_specs=[
                block((inst, width)),
                picked(0, own),
                picked(1, sib),
                block((2, inst)),
                block(pos.shape[1:]),
            ],
            out_specs=[block((2, size, inst)), block((8, inst))],
        ),
        out_shape=(
            jax.ShapeDtypeStruct((y_count, 2, size, inst), jnp.float32),
            jax.ShapeDtypeStruct((y_count, 8, inst), jnp.float32),
        ),
        compiler_params=pltpu.CompilerParams(vmem_limit_bytes=VMEM_LIMIT),
    )(pick, cluster, f_all, own, sib, mask, pos)


def second_pass(pick, cluster, own, sib, mask, pos, kept, lse):
    y_count, _, size, inst = kept.shape
    width = own.shape[2]
    half = jax.ShapeDtypeStruct((y_count, width, inst // 2), jnp.bfloat16)
    return pl.pallas_call(
        grads_kernel,
        grid_spec=pltpu.PrefetchScalarGridSpec(
            num_scalar_prefetch=2,
            grid=(y_count,),
            in_specs=[
                picked(0, own),
                picked(1, sib),
                block((2, inst)),
                block(pos.shape[1:]),
                block((2, size, inst)),
                block((8, inst)),
            ],
            out_specs=[block((width, inst // 2))] * 2,
        ),
        out_shape=(half, half),
        compiler_params=pltpu.CompilerParams(vmem_limit_bytes=VMEM_LIMIT),
    )(pick, cluster, own, sib, mask, pos, kept, lse)


def merge(parts):
    high = parts[0][0:1]
    for part in parts[1:]:
        high = jnp.maximum(high, part[0:1])
    total = sum(part[1:2] * jnp.exp(part[0:1] - high) for part in parts)
    hits = sum(part[2:3] for part in parts)
    return high, total, hits


def lse_kernel(sizes, pos_count, stats, lse_all, loss, held, slots_y, slots_x, slots_z, send_sem, recv_sem):
    y_count, z_count, x_count = sizes
    place = Place(*sizes)
    greet(
        [
            place.device(axis, offset)
            for axis, n in (("y", y_count), ("x", x_count), ("z", z_count))
            for offset in range(1, n)
        ]
    )
    sender = Sender(send_sem, recv_sem)

    def write(ref, values):
        for row, value in enumerate(values):
            ref[row : row + 1, :] = value

    copies = [
        sender.start(stats.at[place.at("y", o)], slots_y.at[o - 1], place.device("y", o))
        for o in range(1, y_count)
    ]
    for copy in copies:
        copy.wait_recv()
    write(held.at[0], merge([stats[place.y]] + [slots_y[o - 1] for o in range(1, y_count)]))
    for stage, (axis, slots) in enumerate((("x", slots_x), ("z", slots_z))):
        n = place.count[axis]
        copies = [
            sender.start(held.at[stage], slots.at[o - 1], place.device(axis, o)) for o in range(1, n)
        ]
        for copy in copies:
            copy.wait_recv()
        merged = merge([held[stage]] + [slots[o - 1] for o in range(1, n)])
        if stage == 0:
            write(held.at[1], merged)
    high, total, hits = merged
    lse = high + jnp.log(total)
    loss[...] = jnp.broadcast_to(lse - hits / pos_count, loss.shape)
    held[2] = jnp.broadcast_to(lse, held.shape[1:])
    lse_all[place.y] = held[2]
    copies = [
        sender.start(held.at[2], lse_all.at[place.y], place.device("y", o))
        for o in range(1, y_count)
    ]
    for copy in copies:
        copy.wait_recv()
    sender.drain()


def exchange_lse(sizes, pos_count, stats):
    y_count, z_count, x_count = sizes
    tile = stats.shape[1:]
    copies = 2 * (y_count - 1) + (x_count - 1) + (z_count - 1)
    return pl.pallas_call(
        functools.partial(lse_kernel, sizes, pos_count),
        out_shape=(
            jax.ShapeDtypeStruct(stats.shape, jnp.float32),
            jax.ShapeDtypeStruct(tile, jnp.float32),
        ),
        in_specs=[pl.BlockSpec(memory_space=pltpu.VMEM)],
        out_specs=[pl.BlockSpec(memory_space=pltpu.VMEM)] * 2,
        scratch_shapes=[
            pltpu.VMEM((3,) + tile, jnp.float32),
            pltpu.VMEM((y_count - 1,) + tile, jnp.float32),
            pltpu.VMEM((x_count - 1,) + tile, jnp.float32),
            pltpu.VMEM((z_count - 1,) + tile, jnp.float32),
            pltpu.SemaphoreType.DMA((copies,)),
            pltpu.SemaphoreType.DMA((copies,)),
        ],
        compiler_params=pltpu.CompilerParams(collective_id=1, has_side_effects=True),
    )(stats)


class Chain:
    def __init__(self, place, axis, sign, half, own, slots, sender):
        self.place, self.axis, self.sign = place, axis, sign
        self.length = reach(place.count[axis], sign, half)
        self.own, self.slots, self.sender = own, slots, sender
        self.step = 0
        self.copies = []

    def advance(self):
        k = self.step
        if k > 0:
            self.copies[-1].wait_recv()
        if k < self.length:
            ref = self.own(self.place.at(self.axis, self.sign * (self.length - k)))
            if k > 0:
                add_into(self.slots.at[k - 1], ref)
                ref = self.slots.at[k - 1]
            self.copies.append(
                self.sender.start(ref, self.slots.at[k], self.place.device(self.axis, self.sign))
            )
        self.step += 1
        return [], self.step > self.length


def add_into(total, term):
    def one(i, carry):
        value = total[i].astype(jnp.float32) + term[i].astype(jnp.float32)
        total[i] = value.astype(total.dtype)
        return carry

    lax.fori_loop(0, total.shape[0], one, 0)


def reduce_kernel(sizes, gx, gz, out, *scratch):
    y_count, z_count, x_count = sizes
    place = Place(*sizes)
    slots = dict(zip(SLOT_NAMES, scratch))
    x_sum, z_sum, y_sum = scratch[len(SLOT_NAMES) : len(SLOT_NAMES) + 3]
    send_sem, recv_sem = scratch[-2:]
    y_half = y_count // 2
    greet([place.device(axis, offset) for axis in "xzy" for offset in (1, -1)])
    sender = Sender(send_sem, recv_sem)

    def halves(half):
        return pl.ds(half * y_half, y_half)

    def chains(name, axis, own):
        return [
            Chain(place, axis, sign, half, functools.partial(own, half), slots[name, sign, half], sender)
            for half, sign in ((0, 1), (1, -1), (1, 1), (0, -1))
            if reach(place.count[axis], sign, half) > 0
        ]

    def landed(name, axis, half):
        n = place.count[axis]
        return [
            slots[name, sign, half].at[reach(n, sign, half) - 1]
            for sign in (1, -1)
            if reach(n, sign, half) > 0
        ]

    run_all(
        chains("z1", "z", lambda half, dest: gz.at[halves(half), dest])
        + chains("x1", "x", lambda half, dest: gx.at[halves(half), :, dest])
    )
    for half in (0, 1):
        for total, first, name, axis in (
            (x_sum, gx.at[:, :, place.x], "x1", "x"),
            (z_sum, gz.at[:, place.z], "z1", "z"),
        ):
            parts = landed(name, axis, half)

            def one(i, carry, total=total, first=first, parts=parts, half=half):
                value = first[half * y_half + i].astype(jnp.float32)
                for part in parts:
                    value = value + part[i].astype(jnp.float32)
                total[half * y_half + i] = value
                return carry

            lax.fori_loop(0, y_half, one, 0)
    run_all(
        chains("x2", "z", lambda half, dest: x_sum.at[halves(half), dest])
        + chains("z2", "x", lambda half, dest: z_sum.at[halves(half), dest])
    )
    for half in (0, 1):
        for lane, first, name, axis in (
            (0, x_sum.at[:, place.z], "x2", "z"),
            (1, z_sum.at[:, place.x], "z2", "x"),
        ):
            parts = landed(name, axis, half)

            def one(i, carry, lane=lane, first=first, parts=parts, half=half):
                value = first[half * y_half + i]
                for part in parts:
                    value = value + part[i]
                y_sum[lane, half * y_half + i] = value
                return carry

            lax.fori_loop(0, y_half, one, 0)
    run_all(chains("y3", "y", lambda half, dest: y_sum.at[half, pl.ds(dest, 1)]))
    for half in (0, 1):
        value = y_sum[half, place.y]
        for part in landed("y3", "y", half):
            value = value + part[0]
        out[half] = value
    sender.drain()


SLOT_NAMES = [
    (name, sign, half)
    for name in ("z1", "x1", "x2", "z2", "y3")
    for half in (0, 1)
    for sign in (1, -1)
]


def reduce_shares(sizes, gx, gz):
    y_count, z_count, x_count = sizes
    lanes = gx.shape[2]
    rows = gx.shape[1] // (z_count * x_count)
    gx = gx.reshape(y_count, z_count, x_count, rows, lanes)
    gz = gz.reshape(y_count, z_count, x_count, rows, lanes)
    y_half = y_count // 2
    pieces = {
        "z1": (z_count, (y_half, x_count, rows, lanes), jnp.bfloat16),
        "x1": (x_count, (y_half, z_count, rows, lanes), jnp.bfloat16),
        "x2": (z_count, (y_half, rows, lanes), jnp.float32),
        "z2": (x_count, (y_half, rows, lanes), jnp.float32),
        "y3": (y_count, (1, rows, lanes), jnp.float32),
    }
    scratch, copies = [], 0
    for name, sign, half in SLOT_NAMES:
        n, shape, dtype = pieces[name]
        steps = reach(n, sign, half)
        copies += steps
        scratch.append(pltpu.VMEM((max(steps, 1),) + shape, dtype))
    scratch += [
        pltpu.VMEM((y_count, z_count, rows, lanes), jnp.float32),
        pltpu.VMEM((y_count, x_count, rows, lanes), jnp.float32),
        pltpu.VMEM((2, y_count, rows, lanes), jnp.float32),
        pltpu.SemaphoreType.DMA((copies,)),
        pltpu.SemaphoreType.DMA((copies,)),
    ]

    return pl.pallas_call(
        functools.partial(reduce_kernel, sizes),
        out_shape=jax.ShapeDtypeStruct((2, rows, lanes), jnp.float32),
        in_specs=[pl.BlockSpec(memory_space=pltpu.VMEM)] * 2,
        out_specs=pl.BlockSpec(memory_space=pltpu.VMEM),
        scratch_shapes=scratch,
        compiler_params=pltpu.CompilerParams(
            collective_id=2, has_side_effects=True, vmem_limit_bytes=VMEM_LIMIT
        ),
    )(gx, gz)


def shards(x_count, feats, weights, shortlist, slot_of, positives):
    y_count = lax.axis_size("dp") // CORES
    lab_count = lax.axis_size("label")
    sizes = (y_count, lab_count // x_count, x_count)
    dp_index, lab_index = lax.axis_index("dp"), lax.axis_index("label")
    core = dp_index % CORES
    stored, size, width = weights.shape
    inst, pos_count = positives.shape
    block_count = inst // BLK
    half_blocks = block_count // 2
    pair = jnp.stack([dp_index, dp_index + 1 - 2 * core]) * lab_count + lab_index
    slots = (pair[:, None] * stored + jnp.arange(stored, dtype=jnp.int32)).reshape(-1)
    ids = jnp.arange(slot_of.shape[0], dtype=jnp.int32)
    clusters = jnp.sum(jnp.where(slots[:, None] == slot_of[None, :], ids[None, :], 0), axis=1)
    lists = shortlist.reshape(y_count, CORES, block_count, -1)
    lists = lax.dynamic_index_in_dim(lists, core, 1, keepdims=False)
    member = jnp.any(lists[:, :, None, :] == clusters[None, None, :, None], axis=3)
    member = member.reshape(y_count, block_count, CORES, stored).astype(jnp.int32)
    chosen = jnp.sum(member[:, :half_blocks], axis=1)
    pick = jnp.sum(chosen * jnp.arange(stored, dtype=jnp.int32), axis=2)
    cluster = jnp.sum(chosen * clusters.reshape(1, CORES, stored), axis=2)
    mask = jnp.sum(member, axis=3).astype(jnp.float32).transpose(0, 2, 1)
    mask = jnp.broadcast_to(mask[..., None], mask.shape + (BLK,)).reshape(y_count, CORES, inst)

    f_all, p_all, sib = gather(sizes, feats, positives.T, weights)
    kept, stats = first_pass(pick, cluster, f_all, weights, sib, mask, p_all)
    lse, loss = exchange_lse(sizes, pos_count, stats)
    gx, gz = second_pass(pick, cluster, weights, sib, mask, p_all, kept, lse)
    grads = reduce_shares(sizes, gx, gz)
    grads = grads.transpose(0, 2, 1).reshape(inst, -1)
    return loss[0], grads.astype(jnp.bfloat16)


def solution(mesh, x_count=X_CHIPS):
    in_specs = (P("dp", None), P(("dp", "label"), None, None), P(), P(), P("dp", None))
    out_specs = (P("dp"), P("dp", "label"))
    return jax.shard_map(
        functools.partial(shards, x_count),
        mesh=mesh,
        in_specs=in_specs,
        out_specs=out_specs,
        check_vma=False,
    )
```

```python
import functools
import heapq
import itertools
import math

import jax
import jax.numpy as jnp
from jax import lax
from jax.experimental import pallas as pl
from jax.experimental.pallas import tpu as pltpu
from jax.sharding import PartitionSpec as P

BLK = 128
CORES = 2
X_CHIPS = 4
VMEM_LIMIT = 60 * 1024 * 1024
NEG_FILL = -1e30
MESH = pl.DeviceIdType.MESH
LINK_RATE = 51e3
LINK_DELAY = 1.5
ISSUE = 0.1
LOGITS_COST = 1.5
GRADS_COST = 1.2


class Place:
    def __init__(self, y_count, z_count, x_count):
        dp, lab = lax.axis_index("dp"), lax.axis_index("label")
        self.dp, self.lab = dp, lab
        self.y, self.core = dp // CORES, dp % CORES
        self.z, self.x = lab // x_count, lab % x_count
        self.count = {"y": y_count, "z": z_count, "x": x_count}
        self.pos = {"y": self.y, "z": self.z, "x": self.x}

    def at(self, axis, offset):
        n = self.count[axis]
        return lax.rem(self.pos[axis] + (offset % n), n)

    def device(self, axis, offset):
        if axis == "core":
            return (self.y * CORES + (1 - self.core), self.lab)
        p = self.at(axis, offset)
        if axis == "y":
            return (p * CORES + self.core, self.lab)
        if axis == "z":
            return (self.dp, p * self.count["x"] + self.x)
        return (self.dp, self.z * self.count["x"] + p)


def greet(devices):
    barrier = pltpu.get_barrier_semaphore()
    for device in devices:
        pl.semaphore_signal(barrier, inc=1, device_id=device, device_id_type=MESH)
    pl.semaphore_wait(barrier, len(devices))


class Engine:
    def __init__(self, place, send_sem, recv_sem):
        self.place, self.send_sem, self.recv_sem = place, send_sem, recv_sem
        self.ids, self.order = itertools.count(), itertools.count()
        self.sent, self.heap, self.ready = [], [], []
        self.free, self.now = {}, 0.0

    def send(self, axis, offset, src, dst, arrived):
        i = next(self.ids)
        copy = pltpu.make_async_remote_copy(
            src_ref=src,
            dst_ref=dst,
            send_sem=self.send_sem.at[i],
            recv_sem=self.recv_sem.at[i],
            device_id=self.place.device(axis, offset),
            device_id_type=MESH,
        )
        copy.start()
        self.sent.append(copy)
        hops, sign, rate = 1, 1, 6 * LINK_RATE
        if axis != "core":
            n = self.place.count[axis]
            offset = offset % n
            sign = 1 if offset <= n // 2 else -1
            hops, rate = min(offset, n - offset), LINK_RATE
        size = math.prod(src.shape) * jnp.dtype(src.dtype).itemsize
        start = max(self.now, self.free.get((axis, sign), 0.0))
        self.free[axis, sign] = start + hops * size / rate
        heapq.heappush(
            self.heap, (self.free[axis, sign] + LINK_DELAY, next(self.order), copy, arrived)
        )
        self.now += ISSUE

    def work(self, cost, run):
        self.ready.append((cost, run))

    def run(self):
        while self.heap or self.ready:
            if self.ready and (not self.heap or self.heap[0][0] > self.now):
                cost, run = self.ready.pop(0)
                run()
                self.now += cost
                continue
            when, _, copy, arrived = heapq.heappop(self.heap)
            self.now = max(self.now, when) + ISSUE
            copy.wait_recv()
            arrived()
        for copy in self.sent:
            copy.wait_send()


def countdown(count, run):
    left = [count]

    def one():
        left[0] -= 1
        if left[0] == 0:
            run()

    return one


def reach(n, sign, half):
    return n // 2 if (sign > 0) == (half == 0) else n // 2 - 1


def spread(engine, axis, half, source, target, arrived):
    place = engine.place
    n = place.count[axis]

    def step(sign, k):
        origin = place.at(axis, -sign * (k - 1))
        src = source() if k == 1 else target(origin)
        engine.send(axis, sign, src, target(origin), lambda: landed(sign, k))

    def landed(sign, k):
        if k + 1 <= reach(n, sign, half):
            step(sign, k + 1)
        arrived(-sign * k % n)

    for sign in (1, -1):
        if reach(n, sign, half) >= 1:
            step(sign, 1)


def add_into(total, term):
    def one(i, carry):
        value = total[i].astype(jnp.float32) + term[i].astype(jnp.float32)
        total[i] = value.astype(total.dtype)
        return carry

    lax.fori_loop(0, total.shape[0], one, 0)


def ring_sum(engine, axis, half, own, slots, total, done):
    place = engine.place
    n = place.count[axis]
    chains = [(sign, reach(n, sign, half)) for sign in (1, -1) if reach(n, sign, half) > 0]

    def finish():
        parts = [slots[sign, half].at[length - 1] for sign, length in chains]
        first = own(place.at(axis, 0))

        def one(i, carry):
            value = first[i].astype(jnp.float32)
            for part in parts:
                value = value + part[i].astype(jnp.float32)
            total[i] = value
            return carry

        lax.fori_loop(0, total.shape[0], one, 0)
        done()

    landed = countdown(len(chains), lambda: engine.work(0.3, finish))

    def step(sign, length, k):
        if k == length:
            landed()
            return
        ref = own(place.at(axis, sign * (length - k)))
        if k > 0:
            add_into(slots[sign, half].at[k - 1], ref)
            engine.now += 0.3
            ref = slots[sign, half].at[k - 1]
        engine.send(axis, sign, ref, slots[sign, half].at[k], lambda: step(sign, length, k + 1))

    for sign, length in chains:
        step(sign, length, 0)


def direct_sum(engine, axis, total, slots, out):
    place = engine.place
    n = place.count[axis]

    def finish():
        value = total[place.at(axis, 0)]
        for o in range(1, n):
            value = value + slots[o - 1]
        out[...] = value

    landed = countdown(n - 1, lambda: engine.work(0.2, finish))
    for o in range(1, n):
        engine.send(axis, o, total.at[place.at(axis, o)], slots.at[o - 1], landed)


def merge(parts):
    high = parts[0][0:1]
    for part in parts[1:]:
        high = jnp.maximum(high, part[0:1])
    total = sum(part[1:2] * jnp.exp(part[0:1] - high) for part in parts)
    hits = sum(part[2:3] for part in parts)
    return high, total, hits


def write(ref, values):
    for row, value in enumerate(values):
        ref[row : row + 1, :] = value


UNIT = 16
SHARES = {"x": 3, "z": 3, "y": 2}


def plan(sizes, inst, width, size, stored, pos_count):
    n = dict(zip("yzx", sizes))
    y, z, x = sizes
    bf, f4 = jnp.bfloat16, jnp.float32
    tile = (8, inst)
    rows = {c: SHARES[c] * UNIT for c in SHARES}
    buffers = {
        "f_all": ((y, inst, width), bf),
        "p_all": ((y, pos_count, inst), jnp.int32),
        "rows_all": ((CORES * stored, size, width), bf),
        "turned": ((CORES * stored, width, size), bf),
        "kept": ((y, CORES, size, inst), f4),
        "hits": ((y, CORES, size, inst), bf),
        "peaks": ((y, CORES) + tile, f4),
        "stats": ((y,) + tile, f4),
        "lse_all": ((y,) + tile, f4),
        "held": ((3,) + tile, f4),
        "stat_y": ((y - 1,) + tile, f4),
        "stat_x": ((x - 1,) + tile, f4),
        "stat_z": ((z - 1,) + tile, f4),
        "g_x": ((y, z, x, rows["x"], BLK), bf),
        "g_z": ((y, z, x, rows["z"], BLK), bf),
        "g_y": ((y, z, x, rows["y"], BLK), bf),
        "x_sum": ((y, z, rows["x"], BLK), f4),
        "xy_sum": ((z, rows["x"], BLK), f4),
        "z_sum": ((y, x, rows["z"], BLK), f4),
        "zx_sum": ((y, rows["z"], BLK), f4),
        "y_sum": ((z, x, rows["y"], BLK), f4),
        "yx_sum": ((z, rows["y"], BLK), f4),
        "last_x": ((z - 1, rows["x"], BLK), f4),
        "last_z": ((y - 1, rows["z"], BLK), f4),
        "last_y": ((z - 1, rows["y"], BLK), f4),
    }
    rings = {
        "x1": ("x", (y // 2, z, rows["x"], BLK), bf),
        "z1": ("z", (y // 2, x, rows["z"], BLK), bf),
        "y1": ("y", (z // 2, x, rows["y"], BLK), bf),
        "x2": ("y", (z // 2, rows["x"], BLK), f4),
        "z2": ("x", (y // 2, rows["z"], BLK), f4),
        "y2": ("x", (z // 2, rows["y"], BLK), f4),
    }
    copies = 1 + 2 * (z - 1) + (y - 1)
    for name, (axis, shape, dtype) in rings.items():
        for sign in (1, -1):
            for half in (0, 1):
                steps = reach(n[axis], sign, half)
                copies += steps
                buffers[name, sign, half] = ((max(steps, 1),) + shape, dtype)
    copies += (y - 1) * (5 + (x - 1) + (z - 1)) + 2 * (y - 1) + (x - 1) + (z - 1)
    return buffers, copies


def step_kernel(sizes, names, pick, cluster, feats, pos, rows, mask, loss, out_x, out_z, out_y, *scratch):
    y_count, z_count, x_count = sizes
    place = Place(*sizes)
    b = dict(zip(names, scratch))
    local_sem, send_sem, recv_sem = scratch[len(names) :]
    inst, width = feats.shape
    stored, size, _ = rows.shape
    pos_count = pos.shape[0]
    y_half, z_half = y_count // 2, z_count // 2
    f_all, p_all, rows_all, turned = b["f_all"], b["p_all"], b["rows_all"], b["turned"]
    kept, hits, peaks, stats, lse_all, held = (
        b[k] for k in ("kept", "hits", "peaks", "stats", "lse_all", "held")
    )
    locals_ = [
        pltpu.make_async_copy(rows, rows_all.at[pl.ds(0, stored)], local_sem.at[0]),
        pltpu.make_async_copy(feats, f_all.at[place.y], local_sem.at[1]),
        pltpu.make_async_copy(pos, p_all.at[place.y], local_sem.at[2]),
    ]
    for copy in locals_:
        copy.start()
    greet(
        [
            place.device(axis, offset)
            for axis, n in (("y", y_count), ("x", x_count), ("z", z_count))
            for offset in range(1, n)
        ]
        + [place.device("core", 1)]
    )
    engine = Engine(place, send_sem, recv_sem)

    def logits_of(offset):
        def run():
            d = place.at("y", offset)

            def one(s, carry):
                logits = lax.dot_general(
                    rows_all[s * stored + pick[d, s]],
                    f_all[d],
                    (((1,), (1,)), ((), ())),
                    preferred_element_type=jnp.float32,
                )
                label = cluster[d, s] * size + lax.broadcasted_iota(jnp.int32, logits.shape, 0)
                hit = p_all[d, 0:1, :] == label
                for p in range(1, pos_count):
                    hit = hit | (p_all[d, p : p + 1, :] == label)
                hits[d, s] = jnp.where(hit, 1.0 / pos_count, 0.0).astype(jnp.bfloat16)
                valid = jnp.where(mask[d, pl.ds(s, 1), :] > 0, logits, NEG_FILL)
                high = jnp.max(valid, axis=0, keepdims=True)
                power = jnp.exp(valid - high)
                kept[d, s] = power
                peak = peaks.at[d, s]
                peak[0:1, :] = high
                peak[1:2, :] = jnp.sum(power, axis=0, keepdims=True)
                peak[2:3, :] = jnp.sum(jnp.where(hit, logits, 0.0), axis=0, keepdims=True)
                return carry

            lax.fori_loop(0, CORES, one, 0)
            stats[d] = jnp.zeros_like(stats[d])
            write(stats.at[d], merge([peaks[d, s] for s in range(CORES)]))
            if offset % y_count:
                engine.send("y", offset, stats.at[d], b["stat_y"].at[offset - 1], stat_landed)
            else:
                stat_landed()

        return run

    def over_y():
        write(
            held.at[0],
            merge([stats[place.y]] + [b["stat_y"][o] for o in range(y_count - 1)]),
        )
        landed = countdown(x_count - 1, lambda: engine.work(0.2, over_x))
        for o in range(1, x_count):
            engine.send("x", o, held.at[0], b["stat_x"].at[o - 1], landed)

    def over_x():
        write(held.at[1], merge([held[0]] + [b["stat_x"][o] for o in range(x_count - 1)]))
        landed = countdown(z_count - 1, lambda: engine.work(0.2, over_z))
        for o in range(1, z_count):
            engine.send("z", o, held.at[1], b["stat_z"].at[o - 1], landed)

    def over_z():
        high, total, found = merge([held[1]] + [b["stat_z"][o] for o in range(z_count - 1)])
        lse = high + jnp.log(total)
        held[2] = jnp.broadcast_to(lse, held.shape[1:])
        landed = countdown(y_count - 1, queue_grads)
        for o in range(1, y_count):
            engine.send("y", o, held.at[2], lse_all.at[place.y], landed)
        loss[...] = jnp.broadcast_to(lse - found / pos_count, loss.shape)
        lse_all[place.y] = held[2]

    stat_landed = countdown(y_count, lambda: engine.work(0.2, over_y))

    def grads_of(half):
        def run():
            def one(i, carry):
                d = half * y_half + i
                shares = None
                lse = lse_all[d, 0:1, :]
                for s in range(CORES):
                    scale = jnp.exp(peaks[d, s, 0:1, :] - lse)
                    dlogit = kept[d, s] * scale - hits[d, s].astype(jnp.float32)
                    term = jnp.dot(
                        turned[s * stored + pick[d, s]],
                        dlogit.astype(jnp.bfloat16),
                        preferred_element_type=jnp.float32,
                    )
                    shares = term if shares is None else shares + term
                shares = shares.astype(jnp.bfloat16).reshape(z_count, x_count, 2 * UNIT, inst)
                b["g_x"][d, :, :, : 2 * UNIT] = shares[..., :BLK]
                b["g_x"][d, :, :, 2 * UNIT :] = shares[:, :, :UNIT, BLK : 2 * BLK]
                b["g_z"][d, :, :, :UNIT] = shares[:, :, UNIT:, BLK : 2 * BLK]
                b["g_z"][d, :, :, UNIT:] = shares[..., 2 * BLK : 3 * BLK]
                b["g_y"][d] = shares[..., 3 * BLK :]
                return carry

            lax.fori_loop(0, y_half, one, 0)
            start_sums(half)

        return run

    def queue_grads():
        for half in (0, 1):
            engine.work(y_half * GRADS_COST, grads_of(half))

    def slots(name):
        return {(sign, half): b[name, sign, half] for sign in (1, -1) for half in (0, 1)}

    def part(half, count):
        return pl.ds(half * count, count)

    def second_x():
        for half in (0, 1):
            ring_sum(
                engine,
                "y",
                half,
                lambda dest, half=half: b["x_sum"].at[dest, part(half, z_half)],
                slots("x2"),
                b["xy_sum"].at[part(half, z_half)],
                last_x,
            )

    last_x = countdown(2, lambda: direct_sum(engine, "z", b["xy_sum"], b["last_x"], out_x))
    last_z = countdown(2, lambda: direct_sum(engine, "y", b["zx_sum"], b["last_z"], out_z))
    last_y = countdown(2, lambda: direct_sum(engine, "z", b["yx_sum"], b["last_y"], out_y))
    first_x = countdown(2, second_x)

    def start_sums(half):
        ring_sum(
            engine,
            "z",
            half,
            lambda dest: b["g_z"].at[part(half, y_half), dest],
            slots("z1"),
            b["z_sum"].at[part(half, y_half)],
            lambda: ring_sum(
                engine,
                "x",
                half,
                lambda dest: b["z_sum"].at[part(half, y_half), dest],
                slots("z2"),
                b["zx_sum"].at[part(half, y_half)],
                last_z,
            ),
        )
        ring_sum(
            engine,
            "x",
            half,
            lambda dest: b["g_x"].at[part(half, y_half), :, dest],
            slots("x1"),
            b["x_sum"].at[part(half, y_half)],
            first_x,
        )
        if half == 0:
            return
        for zh in (0, 1):
            ring_sum(
                engine,
                "y",
                zh,
                lambda dest, zh=zh: b["g_y"].at[dest, part(zh, z_half)],
                slots("y1"),
                b["y_sum"].at[part(zh, z_half)],
                lambda zh=zh: ring_sum(
                    engine,
                    "x",
                    zh,
                    lambda dest: b["y_sum"].at[part(zh, z_half), dest],
                    slots("y2"),
                    b["yx_sum"].at[part(zh, z_half)],
                    last_y,
                ),
            )

    a_part, b_part = inst // 2 // x_count, inst // 4 // z_count
    a_from, b_from = inst // 4, 3 * inst // 4
    c_part = inst // 8
    turn = itertools.count()
    complete = {
        o: countdown(x_count + z_count + 3, lambda o=o: engine.work(LOGITS_COST, logits_of(o)))
        for o in range(1, y_count)
    }

    def cut(origin, start, count):
        return f_all.at[origin, pl.ds(pl.multiple_of(start, 16), count)]

    def a_landed(o):
        origin = place.at("y", o)
        complete[o]()
        spread(
            engine,
            "x",
            next(turn) % 2,
            lambda: cut(origin, a_from + place.x * a_part, a_part),
            lambda p: cut(origin, a_from + p * a_part, a_part),
            lambda _: complete[o](),
        )

    def b_landed(o):
        origin = place.at("y", o)
        complete[o]()
        spread(
            engine,
            "z",
            next(turn) % 2,
            lambda: cut(origin, b_from + place.z * b_part, b_part),
            lambda p: cut(origin, b_from + p * b_part, b_part),
            lambda _: complete[o](),
        )

    def from_feats(start, count):
        return lambda: feats.at[pl.ds(pl.multiple_of(start, 16), count)]

    def turn_rows(base):
        def run():
            def one(i, carry):
                turned[base + i] = rows_all[base + i].T
                return carry

            lax.fori_loop(0, stored, one, 0)

        return run

    def swapped():
        engine.work(LOGITS_COST, logits_of(0))
        engine.work(3.0, turn_rows(stored))

    start = a_from + place.x * a_part
    spread(
        engine, "y", 0, from_feats(start, a_part),
        lambda p, start=start: cut(p, start, a_part), a_landed,
    )
    start = b_from + place.z * b_part
    spread(
        engine, "y", 1, from_feats(start, b_part),
        lambda p, start=start: cut(p, start, b_part), b_landed,
    )
    engine.send("core", 1, rows, rows_all.at[pl.ds(stored, stored)], swapped)
    for o in range(1, y_count):
        engine.send("y", o, pos, p_all.at[place.y], complete[-o % y_count])
    for half in (0, 1):
        spread(
            engine, "y", half, from_feats(half * c_part, c_part),
            lambda p, half=half: cut(p, half * c_part, c_part), lambda o: complete[o](),
        )
    for copy in locals_:
        copy.wait()
    engine.work(3.0, turn_rows(0))
    engine.run()


def step(sizes, pick, cluster, feats, pos, rows, mask):
    inst, width = feats.shape
    stored, size, _ = rows.shape
    buffers, copies = plan(sizes, inst, width, size, stored, pos.shape[0])
    scratch = [pltpu.VMEM(*spec) for spec in buffers.values()]
    scratch += [pltpu.SemaphoreType.DMA((n,)) for n in (3, copies, copies)]
    return pl.pallas_call(
        functools.partial(step_kernel, sizes, list(buffers)),
        out_shape=[jax.ShapeDtypeStruct((8, inst), jnp.float32)]
        + [jax.ShapeDtypeStruct((SHARES[c] * UNIT, BLK), jnp.float32) for c in "xzy"],
        in_specs=[pl.BlockSpec(memory_space=pltpu.SMEM)] * 2
        + [pl.BlockSpec(memory_space=pl.ANY)] * 3
        + [pl.BlockSpec(memory_space=pltpu.VMEM)],
        out_specs=[pl.BlockSpec(memory_space=pltpu.VMEM)] * 4,
        scratch_shapes=scratch,
        compiler_params=pltpu.CompilerParams(
            collective_id=0, has_side_effects=True, vmem_limit_bytes=VMEM_LIMIT
        ),
    )(pick, cluster, feats, pos, rows, mask)


def shards(x_count, feats, weights, shortlist, slot_of, positives):
    y_count = lax.axis_size("dp") // CORES
    lab_count = lax.axis_size("label")
    sizes = (y_count, lab_count // x_count, x_count)
    dp_index, lab_index = lax.axis_index("dp"), lax.axis_index("label")
    core = dp_index % CORES
    stored, size, width = weights.shape
    inst, pos_count = positives.shape
    block_count = inst // BLK
    half_blocks = block_count // 2
    pair = jnp.stack([dp_index, dp_index + 1 - 2 * core]) * lab_count + lab_index
    slots = (pair[:, None] * stored + jnp.arange(stored, dtype=jnp.int32)).reshape(-1)
    ids = jnp.arange(slot_of.shape[0], dtype=jnp.int32)
    clusters = jnp.sum(jnp.where(slots[:, None] == slot_of[None, :], ids[None, :], 0), axis=1)
    lists = shortlist.reshape(y_count, CORES, block_count, -1)
    lists = lax.dynamic_index_in_dim(lists, core, 1, keepdims=False)
    member = jnp.any(lists[:, :, None, :] == clusters[None, None, :, None], axis=3)
    member = member.reshape(y_count, block_count, CORES, stored).astype(jnp.int32)
    chosen = jnp.sum(member[:, :half_blocks], axis=1)
    pick = jnp.sum(chosen * jnp.arange(stored, dtype=jnp.int32), axis=2)
    cluster = jnp.sum(chosen * clusters.reshape(1, CORES, stored), axis=2)
    mask = jnp.sum(member, axis=3).astype(jnp.float32).transpose(0, 2, 1)
    mask = jnp.broadcast_to(mask[..., None], mask.shape + (BLK,)).reshape(y_count, CORES, inst)

    loss, share_x, share_z, share_y = step(sizes, pick, cluster, feats, positives.T, weights, mask)
    lanes = [
        share_x[: 2 * UNIT],
        jnp.concatenate([share_x[2 * UNIT :], share_z[:UNIT]]),
        share_z[UNIT:],
        share_y,
    ]
    grads = jnp.concatenate(lanes, axis=1).T
    return loss[0], grads.astype(jnp.bfloat16)


def solution(mesh, x_count=X_CHIPS):
    in_specs = (P("dp", None), P(("dp", "label"), None, None), P(), P(), P("dp", None))
    out_specs = (P("dp"), P("dp", "label"))
    return jax.shard_map(
        functools.partial(shards, x_count),
        mesh=mesh,
        in_specs=in_specs,
        out_specs=out_specs,
        check_vma=False,
    )
```

```python
import functools
import heapq
import itertools
import math

import jax
import jax.numpy as jnp
from jax import lax
from jax.experimental import pallas as pl
from jax.experimental.pallas import tpu as pltpu
from jax.sharding import PartitionSpec as P

BLK = 128
CORES = 2
X_CHIPS = 4
VMEM_LIMIT = 60 * 1024 * 1024
NEG_FILL = -1e30
MESH = pl.DeviceIdType.MESH
A_PARTS, B_PARTS, C_PARTS = 16, 16, 0
FAR = {"y": 1, "z": 1, "x": 1}
LINK_RATE = 51e3
LINK_DELAY = 2.5
ISSUE = 0.1
LOGITS_COST = 1.5
GRADS_COST = 1.2


class Place:
    def __init__(self, y_count, z_count, x_count):
        dp, lab = lax.axis_index("dp"), lax.axis_index("label")
        self.dp, self.lab = dp, lab
        self.y, self.core = dp // CORES, dp % CORES
        self.z, self.x = lab // x_count, lab % x_count
        self.count = {"y": y_count, "z": z_count, "x": x_count}
        self.pos = {"y": self.y, "z": self.z, "x": self.x}

    def at(self, axis, offset):
        n = self.count[axis]
        return lax.rem(self.pos[axis] + (offset % n), n)

    def device(self, axis, offset):
        if axis == "core":
            return (self.y * CORES + (1 - self.core), self.lab)
        p = self.at(axis, offset)
        if axis == "y":
            return (p * CORES + self.core, self.lab)
        if axis == "z":
            return (self.dp, p * self.count["x"] + self.x)
        return (self.dp, self.z * self.count["x"] + p)


def greet(devices):
    barrier = pltpu.get_barrier_semaphore()
    for device in devices:
        pl.semaphore_signal(barrier, inc=1, device_id=device, device_id_type=MESH)
    pl.semaphore_wait(barrier, len(devices))


class Engine:
    def __init__(self, place, send_sem, recv_sem):
        self.place, self.send_sem, self.recv_sem = place, send_sem, recv_sem
        self.ids, self.order = itertools.count(), itertools.count()
        self.sent, self.heap, self.ready = [], [], []
        self.free, self.now = {}, 0.0

    def send(self, axis, offset, src, dst, arrived):
        i = next(self.ids)
        copy = pltpu.make_async_remote_copy(
            src_ref=src,
            dst_ref=dst,
            send_sem=self.send_sem.at[i],
            recv_sem=self.recv_sem.at[i],
            device_id=self.place.device(axis, offset),
            device_id_type=MESH,
        )
        copy.start()
        self.sent.append(copy)
        hops, sign, rate = 1, 1, 6 * LINK_RATE
        if axis != "core":
            n = self.place.count[axis]
            offset = offset % n
            sign = 1 if offset <= n // 2 else -1
            hops, rate = min(offset, n - offset), LINK_RATE
        size = math.prod(src.shape) * jnp.dtype(src.dtype).itemsize
        start = max(self.now, self.free.get((axis, sign), 0.0))
        self.free[axis, sign] = start + hops * size / rate
        heapq.heappush(
            self.heap, (self.free[axis, sign] + LINK_DELAY, next(self.order), copy, arrived)
        )
        self.now += ISSUE

    def work(self, cost, run):
        self.ready.append((cost, run))

    def run(self):
        while self.heap or self.ready:
            if self.ready and (not self.heap or self.heap[0][0] > self.now):
                cost, run = self.ready.pop(0)
                self.now += cost
                run()
                continue
            when, _, copy, arrived = heapq.heappop(self.heap)
            self.now = max(self.now, when) + ISSUE
            copy.wait_recv()
            arrived()
        for copy in self.sent:
            copy.wait_send()


def countdown(count, run):
    left = [count]

    def one():
        left[0] -= 1
        if left[0] == 0:
            run()

    return one


def reach(n, sign, half):
    return n // 2 if (sign > 0) == (half == 0) else n // 2 - 1


def spread(engine, axis, half, source, target, arrived):
    place = engine.place
    n = place.count[axis]

    far = FAR[axis]

    def pass_on(sign, k):
        origin = place.at(axis, -sign * k)
        src = target(origin) if k else source()
        for hops in range(1, min(far, reach(n, sign, half) - k) + 1):
            engine.send(
                axis, sign * hops, src, target(origin), lambda hops=hops: landed(sign, k + hops)
            )

    def landed(sign, k):
        if k % far == 0:
            pass_on(sign, k)
        arrived(-sign * k % n)

    for sign in (1, -1):
        pass_on(sign, 0)


def add_into(total, term):
    def one(i, carry):
        value = total[i].astype(jnp.float32) + term[i].astype(jnp.float32)
        total[i] = value.astype(total.dtype)
        return carry

    lax.fori_loop(0, total.shape[0], one, 0)


def ring_sum(engine, axis, half, own, slots, total, done):
    place = engine.place
    n = place.count[axis]
    chains = [(sign, reach(n, sign, half)) for sign in (1, -1) if reach(n, sign, half) > 0]

    def finish():
        parts = [slots[sign, half].at[length - 1] for sign, length in chains]
        first = own(place.at(axis, 0))

        def one(i, carry):
            value = first[i].astype(jnp.float32)
            for part in parts:
                value = value + part[i].astype(jnp.float32)
            total[i] = value
            return carry

        lax.fori_loop(0, total.shape[0], one, 0)
        done()

    landed = countdown(len(chains), lambda: engine.work(0.3, finish))

    def step(sign, length, k):
        if k == length:
            landed()
            return
        ref = own(place.at(axis, sign * (length - k)))
        if k > 0:
            add_into(slots[sign, half].at[k - 1], ref)
            engine.now += 0.3
            ref = slots[sign, half].at[k - 1]
        engine.send(axis, sign, ref, slots[sign, half].at[k], lambda: step(sign, length, k + 1))

    for sign, length in chains:
        step(sign, length, 0)


def direct_sum(engine, axis, first, total, slots, out):
    place = engine.place
    n = place.count[axis]

    def finish():
        value = total[place.at(axis, 0)]
        for o in range(1, n):
            value = value + slots[o - 1]
        for place_in, rows_in, lanes_in in spots(first):
            out[rows_in, lanes_in] = value[place_in].astype(out.dtype)

    landed = countdown(n - 1, lambda: engine.work(0.2, finish))
    for o in range(1, n):
        engine.send(axis, o, total.at[place.at(axis, o)], slots.at[o - 1], landed)


def merge(parts, n):
    high = parts[0][0:n]
    for part in parts[1:]:
        high = jnp.maximum(high, part[0:n])
    total = sum(part[n : 2 * n] * jnp.exp(part[0:n] - high) for part in parts)
    hits = sum(part[2 * n : 3 * n] for part in parts)
    return high, total, hits


def write(ref, values):
    row = 0
    for value in values:
        ref[row : row + value.shape[0], :] = value
        row += value.shape[0]


def folded(row):
    return [row[:, i : i + BLK] for i in range(0, row.shape[1], BLK)]


def unfolded(rows):
    return jnp.concatenate([rows[i : i + 1] for i in range(rows.shape[0])], axis=1)


UNIT = 16
UNITS = [(lane, rows) for lane in range(4) for rows in range(2)]
SHARES = {"x": 3, "z": 3, "y": 2}


def units(axis):
    first = {"x": 0, "z": SHARES["x"], "y": SHARES["x"] + SHARES["z"]}[axis]
    return UNITS[first : first + SHARES[axis]]


def spots(axis):
    for i, (lane, rows) in enumerate(units(axis)):
        yield slice(i * UNIT, i * UNIT + UNIT), slice(rows * UNIT, rows * UNIT + UNIT), slice(
            lane * BLK, lane * BLK + BLK
        )


def plan(sizes, inst, width, size, stored, pos_count):
    n = dict(zip("yzx", sizes))
    y, z, x = sizes
    bf, f4 = jnp.bfloat16, jnp.float32
    tile, lse_tile = (4 * inst // BLK, BLK), (8, BLK)
    rows = {c: SHARES[c] * UNIT for c in SHARES}
    buffers = {
        "f_all": ((y, inst, width), bf),
        "p_all": ((y, pos_count, inst), jnp.int32),
        "rows_all": ((CORES * stored, size, width), bf),
        "turned": ((CORES * stored, width, size), bf),
        "kept": ((y, CORES, size, inst), f4),
        "hits": ((y, CORES, size, inst), bf),
        "peaks": ((y, CORES) + tile, f4),
        "stats": ((y,) + tile, f4),
        "lse_all": ((y,) + lse_tile, f4),
        "lse_mine": (lse_tile, f4),
        "held": ((2,) + tile, f4),
        "stat_y": ((y - 1,) + tile, f4),
        "stat_x": ((x - 1,) + tile, f4),
        "stat_z": ((z - 1,) + tile, f4),
        "g_x": ((y, z, x, rows["x"], BLK), bf),
        "g_z": ((y, z, x, rows["z"], BLK), bf),
        "g_y": ((y, z, x, rows["y"], BLK), bf),
        "x_sum": ((y, z, rows["x"], BLK), f4),
        "xy_sum": ((z, rows["x"], BLK), f4),
        "z_sum": ((y, x, rows["z"], BLK), f4),
        "zx_sum": ((y, rows["z"], BLK), f4),
        "y_sum": ((z, x, rows["y"], BLK), f4),
        "yx_sum": ((z, rows["y"], BLK), f4),
        "last_x": ((z - 1, rows["x"], BLK), f4),
        "last_z": ((y - 1, rows["z"], BLK), f4),
        "last_y": ((z - 1, rows["y"], BLK), f4),
    }
    rings = {
        "x1": ("x", (y // 2, z, rows["x"], BLK), bf),
        "z1": ("z", (y // 2, x, rows["z"], BLK), bf),
        "y1": ("y", (z // 2, x, rows["y"], BLK), bf),
        "x2": ("y", (z // 2, rows["x"], BLK), f4),
        "z2": ("x", (y // 2, rows["z"], BLK), f4),
        "y2": ("x", (z // 2, rows["y"], BLK), f4),
    }
    copies = 1 + 2 * (z - 1) + (y - 1)
    for name, (axis, shape, dtype) in rings.items():
        for sign in (1, -1):
            for half in (0, 1):
                steps = reach(n[axis], sign, half)
                copies += steps
                buffers[name, sign, half] = ((max(steps, 1),) + shape, dtype)
    copies += (y - 1) * (5 + (x - 1) + (z - 1)) + 2 * (y - 1) + (x - 1) + (z - 1)
    return buffers, copies


def step_kernel(sizes, names, pick, cluster, feats, pos, rows, mask, loss, out, *scratch):
    y_count, z_count, x_count = sizes
    place = Place(*sizes)
    b = dict(zip(names, scratch))
    local_sem, send_sem, recv_sem = scratch[len(names) :]
    inst, width = feats.shape
    stored, size, _ = rows.shape
    pos_count = pos.shape[0]
    y_half, z_half = y_count // 2, z_count // 2
    f_all, p_all, rows_all, turned = b["f_all"], b["p_all"], b["rows_all"], b["turned"]
    kept, hits, peaks, stats, lse_all, lse_mine, held = (
        b[k] for k in ("kept", "hits", "peaks", "stats", "lse_all", "lse_mine", "held")
    )
    blocks = inst // BLK
    locals_ = [
        pltpu.make_async_copy(rows, rows_all.at[pl.ds(0, stored)], local_sem.at[0]),
        pltpu.make_async_copy(feats, f_all.at[place.y], local_sem.at[1]),
        pltpu.make_async_copy(pos, p_all.at[place.y], local_sem.at[2]),
    ]
    for copy in locals_:
        copy.start()
    greet(
        [
            place.device(axis, offset)
            for axis, n in (("y", y_count), ("x", x_count), ("z", z_count))
            for offset in range(1, n)
        ]
        + [place.device("core", 1)]
    )
    engine = Engine(place, send_sem, recv_sem)

    def logits_of(offset):
        def run():
            d = place.at("y", offset)

            def one(s, carry):
                logits = lax.dot_general(
                    rows_all[s * stored + pick[d, s]],
                    f_all[d],
                    (((1,), (1,)), ((), ())),
                    preferred_element_type=jnp.float32,
                )
                label = cluster[d, s] * size + lax.broadcasted_iota(jnp.int32, logits.shape, 0)
                hit = p_all[d, 0:1, :] == label
                for p in range(1, pos_count):
                    hit = hit | (p_all[d, p : p + 1, :] == label)
                hits[d, s] = jnp.where(hit, 1.0 / pos_count, 0.0).astype(jnp.bfloat16)
                valid = jnp.where(mask[d, pl.ds(s, 1), :] > 0, logits, NEG_FILL)
                high = jnp.max(valid, axis=0, keepdims=True)
                power = jnp.exp(valid - high)
                kept[d, s] = power
                total = jnp.sum(power, axis=0, keepdims=True)
                found = jnp.sum(jnp.where(hit, logits, 0.0), axis=0, keepdims=True)
                write(peaks.at[d, s], folded(high) + folded(total) + folded(found))
                return carry

            lax.fori_loop(0, CORES, one, 0)
            stats[d] = jnp.zeros_like(stats[d])
            write(stats.at[d], merge([peaks[d, s] for s in range(CORES)], blocks))
            if offset % y_count:
                engine.send("y", offset, stats.at[d], b["stat_y"].at[offset - 1], stat_landed)
            else:
                stat_landed()

        return run

    def over_y():
        held[0] = jnp.zeros_like(held[0])
        write(
            held.at[0],
            merge([stats[place.y]] + [b["stat_y"][o] for o in range(y_count - 1)], blocks),
        )
        landed = countdown(x_count - 1, lambda: engine.work(0.2, over_x))
        for o in range(1, x_count):
            engine.send("x", o, held.at[0], b["stat_x"].at[o - 1], landed)

    def over_x():
        held[1] = jnp.zeros_like(held[1])
        write(held.at[1], merge([held[0]] + [b["stat_x"][o] for o in range(x_count - 1)], blocks))
        landed = countdown(z_count - 1, lambda: engine.work(0.2, over_z))
        for o in range(1, z_count):
            engine.send("z", o, held.at[1], b["stat_z"].at[o - 1], landed)

    def over_z():
        high, total, found = merge([held[1]] + [b["stat_z"][o] for o in range(z_count - 1)], blocks)
        lse = high + jnp.log(total)
        lse_mine[...] = jnp.zeros_like(lse_mine)
        write(lse_mine, [lse])
        landed = countdown(y_count - 1, queue_grads)
        for o in range(1, y_count):
            engine.send("y", o, lse_mine, lse_all.at[place.y], landed)
        loss[...] = lse - found / pos_count
        lse_all[place.y] = lse_mine[...]

    stat_landed = countdown(y_count, lambda: engine.work(0.2, over_y))

    def grads_of(half):
        def run():
            def one(i, carry):
                d = half * y_half + i
                shares = None
                lse = lse_all[d][:blocks]
                for s in range(CORES):
                    scale = unfolded(jnp.exp(peaks[d, s][:blocks] - lse))
                    dlogit = kept[d, s] * scale - hits[d, s].astype(jnp.float32)
                    term = jnp.dot(
                        turned[s * stored + pick[d, s]],
                        dlogit.astype(jnp.bfloat16),
                        preferred_element_type=jnp.float32,
                    )
                    shares = term if shares is None else shares + term
                shares = shares.astype(jnp.bfloat16).reshape(z_count, x_count, 2 * UNIT, inst)
                for axis, share in (("x", b["g_x"]), ("z", b["g_z"]), ("y", b["g_y"])):
                    for place_in, rows_in, lanes_in in spots(axis):
                        share[d, :, :, place_in] = shares[:, :, rows_in, lanes_in]
                return carry

            lax.fori_loop(0, y_half, one, 0)
            start_sums(half)

        return run

    def queue_grads():
        for half in (0, 1):
            engine.work(y_half * GRADS_COST, grads_of(half))

    def slots(name):
        return {(sign, half): b[name, sign, half] for sign in (1, -1) for half in (0, 1)}

    def part(half, count):
        return pl.ds(half * count, count)

    def second_x():
        for half in (0, 1):
            ring_sum(
                engine,
                "y",
                half,
                lambda dest, half=half: b["x_sum"].at[dest, part(half, z_half)],
                slots("x2"),
                b["xy_sum"].at[part(half, z_half)],
                last_x,
            )

    last_x = countdown(2, lambda: direct_sum(engine, "z", "x", b["xy_sum"], b["last_x"], out))
    last_z = countdown(2, lambda: direct_sum(engine, "y", "z", b["zx_sum"], b["last_z"], out))
    last_y = countdown(2, lambda: direct_sum(engine, "z", "y", b["yx_sum"], b["last_y"], out))
    first_x = countdown(2, second_x)

    def start_sums(half):
        ring_sum(
            engine,
            "z",
            half,
            lambda dest: b["g_z"].at[part(half, y_half), dest],
            slots("z1"),
            b["z_sum"].at[part(half, y_half)],
            lambda: ring_sum(
                engine,
                "x",
                half,
                lambda dest: b["z_sum"].at[part(half, y_half), dest],
                slots("z2"),
                b["zx_sum"].at[part(half, y_half)],
                last_z,
            ),
        )
        ring_sum(
            engine,
            "x",
            half,
            lambda dest: b["g_x"].at[part(half, y_half), :, dest],
            slots("x1"),
            b["x_sum"].at[part(half, y_half)],
            first_x,
        )
        if half == 0:
            return
        for zh in (0, 1):
            ring_sum(
                engine,
                "y",
                zh,
                lambda dest, zh=zh: b["g_y"].at[dest, part(zh, z_half)],
                slots("y1"),
                b["y_sum"].at[part(zh, z_half)],
                lambda zh=zh: ring_sum(
                    engine,
                    "x",
                    zh,
                    lambda dest: b["y_sum"].at[part(zh, z_half), dest],
                    slots("y2"),
                    b["yx_sum"].at[part(zh, z_half)],
                    last_y,
                ),
            )

    c_part = inst // 32 * C_PARTS // 2
    a_from = 2 * c_part
    a_part, b_part = inst // 32 * A_PARTS // x_count, inst // 32 * B_PARTS // z_count
    b_from = a_from + a_part * x_count
    c_halves = (0, 1) if c_part else ()
    turn = itertools.count()
    complete = {
        o: countdown(x_count + z_count + 1 + len(c_halves), lambda o=o: engine.work(LOGITS_COST, logits_of(o)))
        for o in range(1, y_count)
    }

    def cut(origin, start, count):
        return f_all.at[origin, pl.ds(pl.multiple_of(start, 16), count)]

    def a_landed(o):
        origin = place.at("y", o)
        complete[o]()
        spread(
            engine,
            "x",
            next(turn) % 2,
            lambda: cut(origin, a_from + place.x * a_part, a_part),
            lambda p: cut(origin, a_from + p * a_part, a_part),
            lambda _: complete[o](),
        )

    def b_landed(o):
        origin = place.at("y", o)
        complete[o]()
        spread(
            engine,
            "z",
            next(turn) % 2,
            lambda: cut(origin, b_from + place.z * b_part, b_part),
            lambda p: cut(origin, b_from + p * b_part, b_part),
            lambda _: complete[o](),
        )

    def from_feats(start, count):
        return lambda: feats.at[pl.ds(pl.multiple_of(start, 16), count)]

    def turn_rows(base):
        def run():
            def one(i, carry):
                turned[base + i] = rows_all[base + i].T
                return carry

            lax.fori_loop(0, stored, one, 0)

        return run

    def swapped():
        engine.work(LOGITS_COST, logits_of(0))
        engine.work(3.0, turn_rows(stored))

    start = a_from + place.x * a_part
    spread(
        engine, "y", 0, from_feats(start, a_part),
        lambda p, start=start: cut(p, start, a_part), a_landed,
    )
    start = b_from + place.z * b_part
    spread(
        engine, "y", 1, from_feats(start, b_part),
        lambda p, start=start: cut(p, start, b_part), b_landed,
    )
    engine.send("core", 1, rows, rows_all.at[pl.ds(stored, stored)], swapped)
    for o in range(1, y_count):
        engine.send("y", o, pos, p_all.at[place.y], complete[-o % y_count])
    for half in c_halves:
        spread(
            engine, "y", half, from_feats(half * c_part, c_part),
            lambda p, half=half: cut(p, half * c_part, c_part), lambda o: complete[o](),
        )
    for copy in locals_:
        copy.wait()
    engine.work(3.0, turn_rows(0))
    engine.run()


def step(sizes, pick, cluster, feats, pos, rows, mask):
    inst, width = feats.shape
    stored, size, _ = rows.shape
    buffers, copies = plan(sizes, inst, width, size, stored, pos.shape[0])
    scratch = [pltpu.VMEM(*spec) for spec in buffers.values()]
    scratch += [pltpu.SemaphoreType.DMA((n,)) for n in (3, copies, copies)]
    return pl.pallas_call(
        functools.partial(step_kernel, sizes, list(buffers)),
        out_shape=[
            jax.ShapeDtypeStruct((inst // BLK, BLK), jnp.float32),
            jax.ShapeDtypeStruct((2 * UNIT, inst), jnp.bfloat16),
        ],
        in_specs=[pl.BlockSpec(memory_space=pltpu.SMEM)] * 2
        + [pl.BlockSpec(memory_space=pl.ANY)] * 3
        + [pl.BlockSpec(memory_space=pltpu.VMEM)],
        out_specs=[pl.BlockSpec(memory_space=pltpu.VMEM)] * 2,
        scratch_shapes=scratch,
        compiler_params=pltpu.CompilerParams(
            collective_id=0, has_side_effects=True, vmem_limit_bytes=VMEM_LIMIT
        ),
    )(pick, cluster, feats, pos, rows, mask)


def shards(x_count, feats, weights, shortlist, slot_of, positives):
    y_count = lax.axis_size("dp") // CORES
    lab_count = lax.axis_size("label")
    sizes = (y_count, lab_count // x_count, x_count)
    dp_index, lab_index = lax.axis_index("dp"), lax.axis_index("label")
    core = dp_index % CORES
    stored, size, width = weights.shape
    inst, pos_count = positives.shape
    block_count = inst // BLK
    half_blocks = block_count // 2
    pair = jnp.stack([dp_index, dp_index + 1 - 2 * core]) * lab_count + lab_index
    slots = (pair[:, None] * stored + jnp.arange(stored, dtype=jnp.int32)).reshape(-1)
    ids = jnp.arange(slot_of.shape[0], dtype=jnp.int32)
    clusters = jnp.sum(jnp.where(slots[:, None] == slot_of[None, :], ids[None, :], 0), axis=1)
    lists = shortlist.reshape(y_count, CORES, block_count, -1)
    lists = lax.dynamic_index_in_dim(lists, core, 1, keepdims=False)
    member = jnp.any(lists[:, :, None, :] == clusters[None, None, :, None], axis=3)
    member = member.reshape(y_count, block_count, CORES, stored).astype(jnp.int32)
    chosen = jnp.sum(member[:, :half_blocks], axis=1)
    pick = jnp.sum(chosen * jnp.arange(stored, dtype=jnp.int32), axis=2)
    cluster = jnp.sum(chosen * clusters.reshape(1, CORES, stored), axis=2)
    mask = jnp.sum(member, axis=3).astype(jnp.float32).transpose(0, 2, 1)
    mask = jnp.broadcast_to(mask[..., None], mask.shape + (BLK,)).reshape(y_count, CORES, inst)

    loss, grads = step(sizes, pick, cluster, feats, positives.T, weights, mask)
    return loss.reshape(-1), grads.T


def solution(mesh, x_count=X_CHIPS):
    in_specs = (P("dp", None), P(("dp", "label"), None, None), P(), P(), P("dp", None))
    out_specs = (P("dp"), P("dp", "label"))
    return jax.shard_map(
        functools.partial(shards, x_count),
        mesh=mesh,
        in_specs=in_specs,
        out_specs=out_specs,
        check_vma=False,
    )
```

```python
import functools
import heapq
import itertools
import math

import jax
import jax.numpy as jnp
from jax import lax
from jax.experimental import pallas as pl
from jax.experimental.pallas import tpu as pltpu
from jax.sharding import PartitionSpec as P

BLK = 128
CORES = 2
X_CHIPS = 4
VMEM_LIMIT = 60 * 1024 * 1024
NEG_FILL = -1e30
MESH = pl.DeviceIdType.MESH
A_PARTS, B_PARTS, C_PARTS = 16, 16, 0
FAR = {"y": 1, "z": 1, "x": 1}
LINK_RATE = 51e3
LINK_DELAY = 2.5
ISSUE = 0.1
HITS_COST = 0.7
LOGITS_COST = 1.0
GRADS_COST = 0.8


class Place:
    def __init__(self, y_count, z_count, x_count):
        dp, lab = lax.axis_index("dp"), lax.axis_index("label")
        self.dp, self.lab = dp, lab
        self.y, self.core = dp // CORES, dp % CORES
        self.z, self.x = lab // x_count, lab % x_count
        self.count = {"y": y_count, "z": z_count, "x": x_count}
        self.pos = {"y": self.y, "z": self.z, "x": self.x}

    def at(self, axis, offset):
        n = self.count[axis]
        return lax.rem(self.pos[axis] + (offset % n), n)

    def device(self, axis, offset):
        if axis == "core":
            return (self.y * CORES + (1 - self.core), self.lab)
        p = self.at(axis, offset)
        if axis == "y":
            return (p * CORES + self.core, self.lab)
        if axis == "z":
            return (self.dp, p * self.count["x"] + self.x)
        return (self.dp, self.z * self.count["x"] + p)


def greet(devices):
    barrier = pltpu.get_barrier_semaphore()
    for device in devices:
        pl.semaphore_signal(barrier, inc=1, device_id=device, device_id_type=MESH)
    pl.semaphore_wait(barrier, len(devices))


class Engine:
    def __init__(self, place, send_sem, recv_sem):
        self.place, self.send_sem, self.recv_sem = place, send_sem, recv_sem
        self.ids, self.order = itertools.count(), itertools.count()
        self.sent, self.heap, self.ready = [], [], []
        self.free, self.now = {}, 0.0

    def send(self, axis, offset, src, dst, arrived):
        i = next(self.ids)
        copy = pltpu.make_async_remote_copy(
            src_ref=src,
            dst_ref=dst,
            send_sem=self.send_sem.at[i],
            recv_sem=self.recv_sem.at[i],
            device_id=self.place.device(axis, offset),
            device_id_type=MESH,
        )
        copy.start()
        self.sent.append(copy)
        hops, sign, rate = 1, 1, 6 * LINK_RATE
        if axis != "core":
            n = self.place.count[axis]
            offset = offset % n
            sign = 1 if offset <= n // 2 else -1
            hops, rate = min(offset, n - offset), LINK_RATE
        size = math.prod(src.shape) * jnp.dtype(src.dtype).itemsize
        start = max(self.now, self.free.get((axis, sign), 0.0))
        self.free[axis, sign] = start + hops * size / rate
        heapq.heappush(
            self.heap, (self.free[axis, sign] + LINK_DELAY, next(self.order), copy, arrived)
        )
        self.now += ISSUE

    def work(self, cost, run):
        self.ready.append((cost, run))

    def run(self):
        while self.heap or self.ready:
            if self.ready and (not self.heap or self.heap[0][0] > self.now):
                cost, run = self.ready.pop(0)
                self.now += cost
                run()
                continue
            when, _, copy, arrived = heapq.heappop(self.heap)
            self.now = max(self.now, when) + ISSUE
            copy.wait_recv()
            arrived()
        for copy in self.sent:
            copy.wait_send()


def countdown(count, run):
    left = [count]

    def one():
        left[0] -= 1
        if left[0] == 0:
            run()

    return one


def reach(n, sign, half):
    return n // 2 if (sign > 0) == (half == 0) else n // 2 - 1


def spread(engine, axis, half, source, target, arrived):
    place = engine.place
    n = place.count[axis]

    far = FAR[axis]

    def pass_on(sign, k):
        origin = place.at(axis, -sign * k)
        src = target(origin) if k else source()
        for hops in range(1, min(far, reach(n, sign, half) - k) + 1):
            engine.send(
                axis, sign * hops, src, target(origin), lambda hops=hops: landed(sign, k + hops)
            )

    def landed(sign, k):
        if k % far == 0:
            pass_on(sign, k)
        arrived(-sign * k % n)

    for sign in (1, -1):
        pass_on(sign, 0)


def add_into(total, term):
    def one(i, carry):
        value = total[i].astype(jnp.float32) + term[i].astype(jnp.float32)
        total[i] = value.astype(total.dtype)
        return carry

    lax.fori_loop(0, total.shape[0], one, 0)


def ring_sum(engine, axis, half, own, slots, total, done):
    place = engine.place
    n = place.count[axis]
    chains = [(sign, reach(n, sign, half)) for sign in (1, -1) if reach(n, sign, half) > 0]

    def finish():
        parts = [slots[sign, half].at[length - 1] for sign, length in chains]
        first = own(place.at(axis, 0))

        def one(i, carry):
            value = first[i].astype(jnp.float32)
            for part in parts:
                value = value + part[i].astype(jnp.float32)
            total[i] = value
            return carry

        lax.fori_loop(0, total.shape[0], one, 0)
        done()

    landed = countdown(len(chains), lambda: engine.work(0.3, finish))

    def step(sign, length, k):
        if k == length:
            landed()
            return
        ref = own(place.at(axis, sign * (length - k)))
        if k > 0:
            add_into(slots[sign, half].at[k - 1], ref)
            engine.now += 0.3
            ref = slots[sign, half].at[k - 1]
        engine.send(axis, sign, ref, slots[sign, half].at[k], lambda: step(sign, length, k + 1))

    for sign, length in chains:
        step(sign, length, 0)


def direct_sum(engine, axis, put, total, slots):
    place = engine.place
    n = place.count[axis]

    def finish():
        value = total[place.at(axis, 0)]
        for o in range(1, n):
            value = value + slots[o - 1]
        put(value)

    landed = countdown(n - 1, lambda: engine.work(0.2, finish))
    for o in range(1, n):
        engine.send(axis, o, total.at[place.at(axis, o)], slots.at[o - 1], landed)


def merge(parts, n):
    high = parts[0][0:n]
    for part in parts[1:]:
        high = jnp.maximum(high, part[0:n])
    total = sum(part[n : 2 * n] * jnp.exp(part[0:n] - high) for part in parts)
    hits = sum(part[2 * n : 3 * n] for part in parts)
    return high, total, hits


def write(ref, values):
    row = 0
    for value in values:
        ref[row : row + value.shape[0], :] = value
        row += value.shape[0]


def folded(row):
    return [row[:, i : i + BLK] for i in range(0, row.shape[1], BLK)]


def unfolded(rows):
    return jnp.concatenate([rows[i : i + 1] for i in range(rows.shape[0])], axis=1)


UNIT = 16
UNITS = [(lane, rows) for lane in range(4) for rows in range(2)]
SHARES = {"x": 3, "z": 3, "y": 2}


def units(axis):
    first = {"x": 0, "z": SHARES["x"], "y": SHARES["x"] + SHARES["z"]}[axis]
    return UNITS[first : first + SHARES[axis]]


def spots(axis):
    for i, (lane, rows) in enumerate(units(axis)):
        yield slice(i * UNIT, i * UNIT + UNIT), slice(rows * UNIT, rows * UNIT + UNIT), slice(
            lane * BLK, lane * BLK + BLK
        )


def plan(sizes, inst, width, size, stored, pos_count):
    n = dict(zip("yzx", sizes))
    y, z, x = sizes
    bf, f4 = jnp.bfloat16, jnp.float32
    tile, lse_tile = (4 * inst // BLK, BLK), (8, BLK)
    rows = {c: SHARES[c] * UNIT for c in SHARES}
    buffers = {
        "f_all": ((y, inst, width), bf),
        "p_all": ((y, pos_count, inst), jnp.int32),
        "rows_all": ((CORES * stored, size, width), bf),
        "turned": ((CORES * stored, width, size), bf),
        "kept": ((y, CORES, size, inst), f4),
        "hits": ((y, CORES, size, inst), bf),
        "peaks": ((y, CORES) + tile, f4),
        "stats": ((y,) + tile, f4),
        "lse_all": ((y,) + lse_tile, f4),
        "lse_mine": (lse_tile, f4),
        "held": ((2,) + tile, f4),
        "stat_y": ((y - 1,) + tile, f4),
        "stat_x": ((x - 1,) + tile, f4),
        "stat_z": ((z - 1,) + tile, f4),
        "g_x": ((y, z, x, rows["x"], BLK), bf),
        "g_z": ((y, z, x, rows["z"], BLK), bf),
        "g_y": ((y, z, x, rows["y"], BLK), bf),
        "x_sum": ((y, z, rows["x"], BLK), f4),
        "xy_sum": ((z, rows["x"] // 2, BLK), f4),
        "xz_sum": ((y, rows["x"] // 2, BLK), f4),
        "z_sum": ((y, x, rows["z"], BLK), f4),
        "zx_sum": ((y, rows["z"], BLK), f4),
        "y_sum": ((z, x, rows["y"], BLK), f4),
        "yx_sum": ((z, rows["y"], BLK), f4),
        "last_xy": ((z - 1, rows["x"] // 2, BLK), f4),
        "last_xz": ((y - 1, rows["x"] // 2, BLK), f4),
        "last_z": ((y - 1, rows["z"], BLK), f4),
        "last_y": ((z - 1, rows["y"], BLK), f4),
    }
    rings = {
        "x1": ("x", (y // 2, z, rows["x"], BLK), bf),
        "z1": ("z", (y // 2, x, rows["z"], BLK), bf),
        "y1": ("y", (z // 2, x, rows["y"], BLK), bf),
        "xy2": ("y", (z // 2, rows["x"] // 2, BLK), f4),
        "xz2": ("z", (y // 2, rows["x"] // 2, BLK), f4),
        "z2": ("x", (y // 2, rows["z"], BLK), f4),
        "y2": ("x", (z // 2, rows["y"], BLK), f4),
    }
    copies = 1 + 2 * (z - 1) + 2 * (y - 1)
    for name, (axis, shape, dtype) in rings.items():
        for sign in (1, -1):
            for half in (0, 1):
                steps = reach(n[axis], sign, half)
                copies += steps
                buffers[name, sign, half] = ((max(steps, 1),) + shape, dtype)
    copies += (y - 1) * (5 + (x - 1) + (z - 1)) + 2 * (y - 1) + (x - 1) + (z - 1)
    return buffers, copies


def step_kernel(sizes, names, info, feats, pos, rows, lse_out, found_out, out, *scratch):
    y_count, z_count, x_count = sizes
    place = Place(*sizes)
    b = dict(zip(names, scratch))
    local_sem, send_sem, recv_sem = scratch[len(names) :]
    inst, width = feats.shape
    stored, size, _ = rows.shape
    pos_count = pos.shape[0]
    y_half, z_half = y_count // 2, z_count // 2
    f_all, p_all, rows_all, turned = b["f_all"], b["p_all"], b["rows_all"], b["turned"]
    kept, hits, peaks, stats, lse_all, lse_mine, held = (
        b[k] for k in ("kept", "hits", "peaks", "stats", "lse_all", "lse_mine", "held")
    )
    blocks = inst // BLK
    locals_ = [
        pltpu.make_async_copy(rows, rows_all.at[pl.ds(0, stored)], local_sem.at[0]),
        pltpu.make_async_copy(feats, f_all.at[place.y], local_sem.at[1]),
        pltpu.make_async_copy(pos, p_all.at[place.y], local_sem.at[2]),
    ]
    for copy in locals_:
        copy.start()
    greet(
        [
            place.device(axis, offset)
            for axis, n in (("y", y_count), ("x", x_count), ("z", z_count))
            for offset in range(1, n)
        ]
        + [place.device("core", 1)]
    )
    engine = Engine(place, send_sem, recv_sem)
    fields = 2 + blocks

    def pick(d, s):
        return s * stored + info[d, s * fields]

    def hits_of(offset, done):
        def run():
            d = place.at("y", offset)

            def one(s, carry):
                shape = (size, inst)
                label = info[d, s * fields + 1] * size + lax.broadcasted_iota(jnp.int32, shape, 0)
                hit = p_all[d, 0:1, :] == label
                for p in range(1, pos_count):
                    hit = hit | (p_all[d, p : p + 1, :] == label)
                hits[d, s] = jnp.where(hit, 1.0 / pos_count, 0.0).astype(jnp.bfloat16)
                return carry

            lax.fori_loop(0, CORES, one, 0)
            done()

        return run

    def logits_of(offset):
        def run():
            d = place.at("y", offset)

            def one(s, carry):
                logits = lax.dot_general(
                    rows_all[pick(d, s)],
                    f_all[d],
                    (((1,), (1,)), ((), ())),
                    preferred_element_type=jnp.float32,
                )
                member = jnp.concatenate(
                    [jnp.full((1, BLK), info[d, s * fields + 2 + i]) for i in range(blocks)], axis=1
                )
                valid = jnp.where(member > 0, logits, NEG_FILL)
                high = jnp.max(valid, axis=0, keepdims=True)
                power = jnp.exp(valid - high)
                kept[d, s] = power
                total = jnp.sum(power, axis=0, keepdims=True)
                found = jnp.sum(hits[d, s].astype(jnp.float32) * logits, axis=0, keepdims=True)
                write(peaks.at[d, s], folded(high) + folded(total) + folded(found))
                return carry

            lax.fori_loop(0, CORES, one, 0)
            stats[d] = jnp.zeros_like(stats[d])
            write(stats.at[d], merge([peaks[d, s] for s in range(CORES)], blocks))
            if offset % y_count:
                engine.send("y", offset, stats.at[d], b["stat_y"].at[offset - 1], stat_landed)
            else:
                stat_landed()

        return run

    def over_y():
        held[0] = jnp.zeros_like(held[0])
        write(
            held.at[0],
            merge([stats[place.y]] + [b["stat_y"][o] for o in range(y_count - 1)], blocks),
        )
        landed = countdown(x_count - 1, lambda: engine.work(0.2, over_x))
        for o in range(1, x_count):
            engine.send("x", o, held.at[0], b["stat_x"].at[o - 1], landed)

    def over_x():
        held[1] = jnp.zeros_like(held[1])
        write(held.at[1], merge([held[0]] + [b["stat_x"][o] for o in range(x_count - 1)], blocks))
        landed = countdown(z_count - 1, lambda: engine.work(0.2, over_z))
        for o in range(1, z_count):
            engine.send("z", o, held.at[1], b["stat_z"].at[o - 1], landed)

    def over_z():
        high, total, found = merge([held[1]] + [b["stat_z"][o] for o in range(z_count - 1)], blocks)
        lse = high + jnp.log(total)
        lse_mine[...] = jnp.zeros_like(lse_mine)
        write(lse_mine, [lse])
        landed = countdown(y_count - 1, queue_grads)
        for o in range(1, y_count):
            engine.send("y", o, lse_mine, lse_all.at[place.y], landed)
        lse_out[...] = lse
        found_out[...] = found
        lse_all[place.y] = lse_mine[...]

    stat_landed = countdown(y_count, lambda: engine.work(0.2, over_y))

    def grads_of(half):
        def run():
            def one(i, carry):
                d = half * y_half + i
                shares = None
                lse = lse_all[d][:blocks]
                for s in range(CORES):
                    scale = unfolded(jnp.exp(peaks[d, s][:blocks] - lse))
                    dlogit = kept[d, s] * scale - hits[d, s].astype(jnp.float32)
                    term = jnp.dot(
                        turned[pick(d, s)],
                        dlogit.astype(jnp.bfloat16),
                        preferred_element_type=jnp.float32,
                    )
                    shares = term if shares is None else shares + term
                shares = shares.astype(jnp.bfloat16).reshape(z_count, x_count, 2 * UNIT, inst)
                for axis, share in (("x", b["g_x"]), ("z", b["g_z"]), ("y", b["g_y"])):
                    for place_in, rows_in, lanes_in in spots(axis):
                        share[d, :, :, place_in] = shares[:, :, rows_in, lanes_in]
                return carry

            lax.fori_loop(0, y_half, one, 0)
            start_sums(half)

        return run

    def queue_grads():
        for half in (0, 1):
            engine.work(y_half * GRADS_COST, grads_of(half))

    def slots(name):
        return {(sign, half): b[name, sign, half] for sign in (1, -1) for half in (0, 1)}

    def part(half, count):
        return pl.ds(half * count, count)

    def put(axis, start):
        def run(value):
            stop = start + value.shape[0]
            for place_in, rows_in, lanes_in in spots(axis):
                low, high = max(place_in.start, start), min(place_in.stop, stop)
                if low < high:
                    first = rows_in.start + low - place_in.start
                    out[first : first + high - low, lanes_in] = value[low - start : high - start]

        return run

    def put_x(which):
        return put("x", which * x_part)

    x_part = SHARES["x"] * UNIT // 2

    def second_xy():
        for half in (0, 1):
            ring_sum(
                engine,
                "y",
                half,
                lambda dest, half=half: b["x_sum"].at[dest, part(half, z_half), :x_part],
                slots("xy2"),
                b["xy_sum"].at[part(half, z_half)],
                last_xy,
            )

    def second_xz(half):
        ring_sum(
            engine,
            "z",
            half,
            lambda dest: b["x_sum"].at[part(half, y_half), dest, x_part:],
            slots("xz2"),
            b["xz_sum"].at[part(half, y_half)],
            last_xz,
        )
        first_x()

    last_xy = countdown(2, lambda: direct_sum(engine, "z", put_x(0), b["xy_sum"], b["last_xy"]))
    last_xz = countdown(2, lambda: direct_sum(engine, "y", put_x(1), b["xz_sum"], b["last_xz"]))
    last_z = countdown(2, lambda: direct_sum(engine, "y", put("z", 0), b["zx_sum"], b["last_z"]))
    last_y = countdown(2, lambda: direct_sum(engine, "z", put("y", 0), b["yx_sum"], b["last_y"]))
    first_x = countdown(2, second_xy)

    def start_sums(half):
        ring_sum(
            engine,
            "z",
            half,
            lambda dest: b["g_z"].at[part(half, y_half), dest],
            slots("z1"),
            b["z_sum"].at[part(half, y_half)],
            lambda: ring_sum(
                engine,
                "x",
                half,
                lambda dest: b["z_sum"].at[part(half, y_half), dest],
                slots("z2"),
                b["zx_sum"].at[part(half, y_half)],
                last_z,
            ),
        )
        ring_sum(
            engine,
            "x",
            half,
            lambda dest: b["g_x"].at[part(half, y_half), :, dest],
            slots("x1"),
            b["x_sum"].at[part(half, y_half)],
            lambda: second_xz(half),
        )
        if half == 0:
            return
        for zh in (0, 1):
            ring_sum(
                engine,
                "y",
                zh,
                lambda dest, zh=zh: b["g_y"].at[dest, part(zh, z_half)],
                slots("y1"),
                b["y_sum"].at[part(zh, z_half)],
                lambda zh=zh: ring_sum(
                    engine,
                    "x",
                    zh,
                    lambda dest: b["y_sum"].at[part(zh, z_half), dest],
                    slots("y2"),
                    b["yx_sum"].at[part(zh, z_half)],
                    last_y,
                ),
            )

    c_part = inst // 32 * C_PARTS // 2
    a_from = 2 * c_part
    a_part, b_part = inst // 32 * A_PARTS // x_count, inst // 32 * B_PARTS // z_count
    b_from = a_from + a_part * x_count
    c_halves = (0, 1) if c_part else ()
    turn_a, turn_b = itertools.count(), itertools.count()
    complete = {
        o: countdown(x_count + z_count + 1 + len(c_halves), lambda o=o: engine.work(LOGITS_COST, logits_of(o)))
        for o in range(1, y_count)
    }

    complete[0] = countdown(2, lambda: engine.work(LOGITS_COST, logits_of(0)))

    def hits_next(o):
        return lambda: engine.work(HITS_COST, hits_of(o, complete[o]))

    def cut(origin, start, count):
        return f_all.at[origin, pl.ds(pl.multiple_of(start, 16), count)]

    def a_landed(o):
        origin = place.at("y", o)
        complete[o]()
        spread(
            engine,
            "x",
            next(turn_a) % 2,
            lambda: cut(origin, a_from + place.x * a_part, a_part),
            lambda p: cut(origin, a_from + p * a_part, a_part),
            lambda _: complete[o](),
        )

    def b_landed(o):
        origin = place.at("y", o)
        complete[o]()
        spread(
            engine,
            "z",
            next(turn_b) % 2,
            lambda: cut(origin, b_from + place.z * b_part, b_part),
            lambda p: cut(origin, b_from + p * b_part, b_part),
            lambda _: complete[o](),
        )

    def from_feats(start, count):
        return lambda: feats.at[pl.ds(pl.multiple_of(start, 16), count)]

    def turn_rows(base):
        def run():
            def one(i, carry):
                turned[base + i] = rows_all[base + i].T
                return carry

            lax.fori_loop(0, stored, one, 0)

        return run

    def swapped():
        complete[0]()
        engine.work(3.0, turn_rows(stored))

    start = b_from + place.z * b_part
    spread(
        engine, "y", 1, from_feats(start, b_part),
        lambda p, start=start: cut(p, start, b_part), b_landed,
    )
    start = a_from + place.x * a_part
    spread(
        engine, "y", 0, from_feats(start, a_part),
        lambda p, start=start: cut(p, start, a_part), a_landed,
    )
    engine.send("core", 1, rows, rows_all.at[pl.ds(stored, stored)], swapped)
    for o in range(1, y_count):
        engine.send("y", o, pos, p_all.at[place.y], hits_next(-o % y_count))
    for half in c_halves:
        spread(
            engine, "y", half, from_feats(half * c_part, c_part),
            lambda p, half=half: cut(p, half * c_part, c_part), lambda o: complete[o](),
        )
    for copy in locals_:
        copy.wait()
    hits_next(0)()
    engine.work(3.0, turn_rows(0))
    engine.run()


def step(sizes, info, feats, pos, rows):
    inst, width = feats.shape
    stored, size, _ = rows.shape
    buffers, copies = plan(sizes, inst, width, size, stored, pos.shape[0])
    scratch = [pltpu.VMEM(*spec) for spec in buffers.values()]
    scratch += [pltpu.SemaphoreType.DMA((n,)) for n in (3, copies, copies)]
    return pl.pallas_call(
        functools.partial(step_kernel, sizes, list(buffers)),
        out_shape=[
            jax.ShapeDtypeStruct((inst // BLK, BLK), jnp.float32),
            jax.ShapeDtypeStruct((inst // BLK, BLK), jnp.float32),
            jax.ShapeDtypeStruct((2 * UNIT, inst), jnp.float32),
        ],
        in_specs=[pl.BlockSpec(memory_space=pltpu.SMEM)] + [pl.BlockSpec(memory_space=pl.ANY)] * 3,
        out_specs=[pl.BlockSpec(memory_space=pltpu.VMEM)] * 3,
        scratch_shapes=scratch,
        compiler_params=pltpu.CompilerParams(
            collective_id=0, has_side_effects=True, vmem_limit_bytes=VMEM_LIMIT
        ),
    )(info, feats, pos, rows)


def shards(x_count, feats, weights, shortlist, slot_of, positives):
    y_count = lax.axis_size("dp") // CORES
    lab_count = lax.axis_size("label")
    sizes = (y_count, lab_count // x_count, x_count)
    dp_index, lab_index = lax.axis_index("dp"), lax.axis_index("label")
    core = dp_index % CORES
    stored, size, width = weights.shape
    inst, pos_count = positives.shape
    block_count = inst // BLK
    half_blocks = block_count // 2
    pair = jnp.stack([dp_index, dp_index + 1 - 2 * core]) * lab_count + lab_index
    slots = (pair[:, None] * stored + jnp.arange(stored, dtype=jnp.int32)).reshape(-1)
    ids = jnp.arange(slot_of.shape[0], dtype=jnp.int32)
    clusters = jnp.sum(jnp.where(slots[:, None] == slot_of[None, :], ids[None, :], 0), axis=1)
    member = jnp.any(shortlist[:, None, :] == clusters[None, :, None], axis=2)
    member = member.reshape(y_count, CORES, block_count, CORES, stored)
    member = lax.dynamic_index_in_dim(member, core, 1, keepdims=False).astype(jnp.int32)
    chosen = jnp.sum(member[:, :half_blocks], axis=1)
    pick = jnp.sum(chosen * jnp.arange(stored, dtype=jnp.int32), axis=2)
    cluster = jnp.sum(chosen * clusters.reshape(1, CORES, stored), axis=2)
    blocks = jnp.sum(member, axis=3).transpose(0, 2, 1)
    info = jnp.concatenate([pick[..., None], cluster[..., None], blocks], axis=2)
    lse, found, grads = step(sizes, info.reshape(y_count, -1), feats, positives.T, weights)
    return (lse - found).reshape(-1), grads.astype(jnp.bfloat16).T


def solution(mesh, x_count=X_CHIPS):
    in_specs = (P("dp", None), P(("dp", "label"), None, None), P(), P(), P("dp", None))
    out_specs = (P("dp"), P("dp", "label"))
    return jax.shard_map(
        functools.partial(shards, x_count),
        mesh=mesh,
        in_specs=in_specs,
        out_specs=out_specs,
        check_vma=False,
    )
```

```python
import functools
import heapq
import itertools
import math

import jax
import jax.numpy as jnp
from jax import lax
from jax.experimental import pallas as pl
from jax.experimental.pallas import tpu as pltpu
from jax.sharding import PartitionSpec as P

BLK = 128
CORES = 2
X_CHIPS = 4
VMEM_LIMIT = 60 * 1024 * 1024
NEG_FILL = -1e30
MESH = pl.DeviceIdType.MESH
A_PARTS, B_PARTS, C_PARTS = 16, 16, 0
LINK_RATE = 51e3
LINK_DELAY = 2.5
ISSUE = 0.1
HITS_COST = 0.7
LOGITS_COST = 1.0
GRADS_COST = 0.8


class Place:
    def __init__(self, y_count, z_count, x_count):
        dp, lab = lax.axis_index("dp"), lax.axis_index("label")
        self.dp, self.lab = dp, lab
        self.y, self.core = dp // CORES, dp % CORES
        self.z, self.x = lab // x_count, lab % x_count
        self.count = {"y": y_count, "z": z_count, "x": x_count}
        self.pos = {"y": self.y, "z": self.z, "x": self.x}

    def at(self, axis, offset):
        n = self.count[axis]
        return lax.rem(self.pos[axis] + (offset % n), n)

    def device(self, axis, offset):
        if axis == "core":
            return (self.y * CORES + (1 - self.core), self.lab)
        p = self.at(axis, offset)
        if axis == "y":
            return (p * CORES + self.core, self.lab)
        if axis == "z":
            return (self.dp, p * self.count["x"] + self.x)
        return (self.dp, self.z * self.count["x"] + p)


def greet(devices):
    barrier = pltpu.get_barrier_semaphore()
    for device in devices:
        pl.semaphore_signal(barrier, inc=1, device_id=device, device_id_type=MESH)
    pl.semaphore_wait(barrier, len(devices))


class Engine:
    def __init__(self, place, send_sem, recv_sem):
        self.place, self.send_sem, self.recv_sem = place, send_sem, recv_sem
        self.ids, self.order = itertools.count(), itertools.count()
        self.sent, self.heap, self.ready = [], [], []
        self.free, self.now = {}, 0.0

    def send(self, axis, offset, src, dst, arrived):
        i = next(self.ids)
        copy = pltpu.make_async_remote_copy(
            src_ref=src,
            dst_ref=dst,
            send_sem=self.send_sem.at[i],
            recv_sem=self.recv_sem.at[i],
            device_id=self.place.device(axis, offset),
            device_id_type=MESH,
        )
        copy.start()
        self.sent.append(copy)
        hops, sign, rate = 1, 1, 6 * LINK_RATE
        if axis != "core":
            n = self.place.count[axis]
            offset = offset % n
            sign = 1 if offset <= n // 2 else -1
            hops, rate = min(offset, n - offset), LINK_RATE
        size = math.prod(src.shape) * jnp.dtype(src.dtype).itemsize
        start = max(self.now, self.free.get((axis, sign), 0.0))
        self.free[axis, sign] = start + hops * size / rate
        heapq.heappush(
            self.heap, (self.free[axis, sign] + LINK_DELAY, next(self.order), copy, arrived)
        )
        self.now += ISSUE

    def work(self, cost, run):
        self.ready.append((cost, run))

    def run(self):
        while self.heap or self.ready:
            if self.ready and (not self.heap or self.heap[0][0] > self.now):
                cost, run = self.ready.pop(0)
                self.now += cost
                run()
                continue
            when, _, copy, arrived = heapq.heappop(self.heap)
            self.now = max(self.now, when) + ISSUE
            copy.wait_recv()
            arrived()
        for copy in self.sent:
            copy.wait_send()


def countdown(count, run):
    left = [count]

    def one():
        left[0] -= 1
        if left[0] == 0:
            run()

    return one


def reach(n, sign, half):
    return n // 2 if (sign > 0) == (half == 0) else n // 2 - 1


def spread(engine, axis, half, source, target, arrived):
    place = engine.place
    n = place.count[axis]

    def pass_on(sign, k):
        if k < reach(n, sign, half):
            origin = place.at(axis, -sign * k)
            src = target(origin) if k else source()
            engine.send(axis, sign, src, target(origin), lambda: landed(sign, k + 1))

    def landed(sign, k):
        pass_on(sign, k)
        arrived(-sign * k % n)

    for sign in (1, -1):
        pass_on(sign, 0)


def add_into(total, term):
    def one(i, carry):
        value = total[i].astype(jnp.float32) + term[i].astype(jnp.float32)
        total[i] = value.astype(total.dtype)
        return carry

    lax.fori_loop(0, total.shape[0], one, 0)


def ring_sum(engine, axis, half, own, slots, total, done):
    place = engine.place
    n = place.count[axis]
    chains = [(sign, reach(n, sign, half)) for sign in (1, -1) if reach(n, sign, half) > 0]

    def finish():
        parts = [slots[sign, half].at[length - 1] for sign, length in chains]
        first = own(place.at(axis, 0))

        def one(i, carry):
            value = first[i].astype(jnp.float32)
            for part in parts:
                value = value + part[i].astype(jnp.float32)
            total[i] = value
            return carry

        lax.fori_loop(0, total.shape[0], one, 0)
        done()

    landed = countdown(len(chains), lambda: engine.work(0.3, finish))

    def step(sign, length, k):
        if k == length:
            landed()
            return
        ref = own(place.at(axis, sign * (length - k)))
        if k > 0:
            add_into(slots[sign, half].at[k - 1], ref)
            engine.now += 0.3
            ref = slots[sign, half].at[k - 1]
        engine.send(axis, sign, ref, slots[sign, half].at[k], lambda: step(sign, length, k + 1))

    for sign, length in chains:
        step(sign, length, 0)


def hub_sum(engine, axis, half, own, slots, total, done):
    place = engine.place
    n = place.count[axis]
    chains = [(sign, reach(n, sign, half)) for sign in (1, -1) if reach(n, sign, half) > 0]
    near, hub, third, fourth = range(4)

    def finish():
        first = own(place.at(axis, 0))
        parts = [
            slots[sign, half].at[k] for sign, length in chains for k in range(min(length, 2))
        ]

        def one(i, carry):
            value = first[i]
            for part in parts:
                value = value + part[i]
            total[i] = value
            return carry

        lax.fori_loop(0, total.shape[0], one, 0)
        done()

    landed = countdown(
        sum(min(length, 2) for _, length in chains), lambda: engine.work(0.3, finish)
    )

    def start(sign, length):
        inbox = slots[sign, half]

        def relay():
            ref = own(place.at(axis, 2 * sign))
            for k in range(fourth, hub, -1):
                if k < length:
                    add_into(inbox.at[k], ref)
                    ref = inbox.at[k]
                    engine.now += 0.2
            engine.send(axis, 2 * sign, ref, inbox.at[hub], landed)

        collected = countdown(length - 2, relay) if length > 2 else None
        for k in range(fourth, hub, -1):
            if k < length:
                engine.send(axis, (k - 1) * sign, own(place.at(axis, (k + 1) * sign)), inbox.at[k], collected)
        if length == 2:
            relay()
        engine.send(axis, sign, own(place.at(axis, sign)), inbox.at[near], landed)

    for sign, length in chains:
        start(sign, length)


def direct_sum(engine, axis, put, total, slots):
    place = engine.place
    n = place.count[axis]

    def finish():
        value = total[place.at(axis, 0)]
        for o in range(1, n):
            value = value + slots[o - 1]
        put(value)

    landed = countdown(n - 1, lambda: engine.work(0.2, finish))
    for o in range(1, n):
        engine.send(axis, o, total.at[place.at(axis, o)], slots.at[o - 1], landed)


def merge(parts, n):
    high = parts[0][0:n]
    for part in parts[1:]:
        high = jnp.maximum(high, part[0:n])
    total = sum(part[n : 2 * n] * jnp.exp(part[0:n] - high) for part in parts)
    hits = sum(part[2 * n : 3 * n] for part in parts)
    return high, total, hits


def write(ref, values):
    row = 0
    for value in values:
        ref[row : row + value.shape[0], :] = value
        row += value.shape[0]


def folded(row):
    return [row[:, i : i + BLK] for i in range(0, row.shape[1], BLK)]


def unfolded(rows):
    return jnp.concatenate([rows[i : i + 1] for i in range(rows.shape[0])], axis=1)


UNIT = 16
UNITS = [(lane, rows) for lane in range(4) for rows in range(2)]
SHARES = {"x": 3, "z": 3, "y": 2}


def units(axis):
    first = {"x": 0, "z": SHARES["x"], "y": SHARES["x"] + SHARES["z"]}[axis]
    return UNITS[first : first + SHARES[axis]]


def spots(axis):
    for i, (lane, rows) in enumerate(units(axis)):
        yield slice(i * UNIT, i * UNIT + UNIT), slice(rows * UNIT, rows * UNIT + UNIT), slice(
            lane * BLK, lane * BLK + BLK
        )


def plan(sizes, inst, width, size, stored, pos_count):
    n = dict(zip("yzx", sizes))
    y, z, x = sizes
    bf, f4 = jnp.bfloat16, jnp.float32
    tile, lse_tile = (4 * inst // BLK, BLK), (8, BLK)
    rows = {c: SHARES[c] * UNIT for c in SHARES}
    buffers = {
        "f_all": ((y, inst, width), bf),
        "p_all": ((y, pos_count, inst), jnp.int32),
        "rows_all": ((CORES * stored, size, width), bf),
        "turned": ((CORES * stored, width, size), bf),
        "kept": ((y, CORES, size, inst), f4),
        "hits": ((y, CORES, size, inst), bf),
        "peaks": ((y, CORES) + tile, f4),
        "stats": ((y,) + tile, f4),
        "lse_all": ((y,) + lse_tile, f4),
        "lse_mine": (lse_tile, f4),
        "held": ((2,) + tile, f4),
        "stat_y": ((y - 1,) + tile, f4),
        "stat_x": ((x - 1,) + tile, f4),
        "stat_z": ((z - 1,) + tile, f4),
        "g_x": ((y, z, x, rows["x"], BLK), bf),
        "g_z": ((y, z, x, rows["z"], BLK), bf),
        "g_y": ((y, z, x, rows["y"], BLK), bf),
        "x_sum": ((y, z, rows["x"], BLK), f4),
        "xy_sum": ((z, rows["x"] // 2, BLK), f4),
        "xz_sum": ((y, rows["x"] // 2, BLK), f4),
        "z_sum": ((y, x, rows["z"], BLK), f4),
        "zx_sum": ((y, rows["z"], BLK), f4),
        "y_sum": ((z, x, rows["y"], BLK), f4),
        "yx_sum": ((z, rows["y"], BLK), f4),
        "last_xy": ((z - 1, rows["x"] // 2, BLK), f4),
        "last_xz": ((y - 1, rows["x"] // 2, BLK), f4),
        "last_z": ((y - 1, rows["z"], BLK), f4),
        "last_y": ((z - 1, rows["y"], BLK), f4),
    }
    rings = {
        "x1": ("x", (y // 2, z, rows["x"], BLK), bf),
        "z1": ("z", (y // 2, x, rows["z"], BLK), bf),
        "y1": ("y", (z // 2, x, rows["y"], BLK), bf),
        "xy2": ("y", (z // 2, rows["x"] // 2, BLK), f4),
        "xz2": ("z", (y // 2, rows["x"] // 2, BLK), f4),
        "z2": ("x", (y // 2, rows["z"], BLK), f4),
        "y2": ("x", (z // 2, rows["y"], BLK), f4),
    }
    copies = 1 + 2 * (z - 1) + 2 * (y - 1)
    for name, (axis, shape, dtype) in rings.items():
        for sign in (1, -1):
            for half in (0, 1):
                steps = reach(n[axis], sign, half)
                copies += steps
                buffers[name, sign, half] = ((max(steps, 1),) + shape, dtype)
    copies += (y - 1) * (5 + (x - 1) + (z - 1)) + 2 * (y - 1) + (x - 1) + (z - 1)
    return buffers, copies


def step_kernel(sizes, names, info, feats, pos, rows, lse_out, found_out, out, *scratch):
    y_count, z_count, x_count = sizes
    place = Place(*sizes)
    b = dict(zip(names, scratch))
    local_sem, send_sem, recv_sem = scratch[len(names) :]
    inst, width = feats.shape
    stored, size, _ = rows.shape
    pos_count = pos.shape[0]
    y_half, z_half = y_count // 2, z_count // 2
    f_all, p_all, rows_all, turned = b["f_all"], b["p_all"], b["rows_all"], b["turned"]
    kept, hits, peaks, stats, lse_all, lse_mine, held = (
        b[k] for k in ("kept", "hits", "peaks", "stats", "lse_all", "lse_mine", "held")
    )
    blocks = inst // BLK
    locals_ = [
        pltpu.make_async_copy(rows, rows_all.at[pl.ds(0, stored)], local_sem.at[0]),
        pltpu.make_async_copy(feats, f_all.at[place.y], local_sem.at[1]),
        pltpu.make_async_copy(pos, p_all.at[place.y], local_sem.at[2]),
    ]
    for copy in locals_:
        copy.start()
    greet(
        [
            place.device(axis, offset)
            for axis, n in (("y", y_count), ("x", x_count), ("z", z_count))
            for offset in range(1, n)
        ]
        + [place.device("core", 1)]
    )
    engine = Engine(place, send_sem, recv_sem)
    fields = 2 + blocks

    def pick(d, s):
        return s * stored + info[d, s * fields]

    def hits_of(offset, done):
        def run():
            d = place.at("y", offset)

            def one(s, carry):
                shape = (size, inst)
                label = info[d, s * fields + 1] * size + lax.broadcasted_iota(jnp.int32, shape, 0)
                hit = p_all[d, 0:1, :] == label
                for p in range(1, pos_count):
                    hit = hit | (p_all[d, p : p + 1, :] == label)
                hits[d, s] = jnp.where(hit, 1.0 / pos_count, 0.0).astype(jnp.bfloat16)
                return carry

            lax.fori_loop(0, CORES, one, 0)
            done()

        return run

    def logits_of(offset):
        def run():
            d = place.at("y", offset)

            def one(s, carry):
                logits = lax.dot_general(
                    rows_all[pick(d, s)],
                    f_all[d],
                    (((1,), (1,)), ((), ())),
                    preferred_element_type=jnp.float32,
                )
                member = jnp.concatenate(
                    [jnp.full((1, BLK), info[d, s * fields + 2 + i]) for i in range(blocks)], axis=1
                )
                valid = jnp.where(member > 0, logits, NEG_FILL)
                high = jnp.max(valid, axis=0, keepdims=True)
                power = jnp.exp(valid - high)
                kept[d, s] = power
                total = jnp.sum(power, axis=0, keepdims=True)
                found = jnp.sum(hits[d, s].astype(jnp.float32) * logits, axis=0, keepdims=True)
                write(peaks.at[d, s], folded(high) + folded(total) + folded(found))
                return carry

            lax.fori_loop(0, CORES, one, 0)
            stats[d] = jnp.zeros_like(stats[d])
            write(stats.at[d], merge([peaks[d, s] for s in range(CORES)], blocks))
            if offset % y_count:
                engine.send("y", offset, stats.at[d], b["stat_y"].at[offset - 1], stat_landed)
            else:
                stat_landed()

        return run

    def over_y():
        held[0] = jnp.zeros_like(held[0])
        write(
            held.at[0],
            merge([stats[place.y]] + [b["stat_y"][o] for o in range(y_count - 1)], blocks),
        )
        landed = countdown(x_count - 1, lambda: engine.work(0.2, over_x))
        for o in range(1, x_count):
            engine.send("x", o, held.at[0], b["stat_x"].at[o - 1], landed)

    def over_x():
        held[1] = jnp.zeros_like(held[1])
        write(held.at[1], merge([held[0]] + [b["stat_x"][o] for o in range(x_count - 1)], blocks))
        landed = countdown(z_count - 1, lambda: engine.work(0.2, over_z))
        for o in range(1, z_count):
            engine.send("z", o, held.at[1], b["stat_z"].at[o - 1], landed)

    def over_z():
        high, total, found = merge([held[1]] + [b["stat_z"][o] for o in range(z_count - 1)], blocks)
        lse = high + jnp.log(total)
        lse_mine[...] = jnp.zeros_like(lse_mine)
        write(lse_mine, [lse])
        landed = countdown(y_count - 1, queue_grads)
        for o in range(1, y_count):
            engine.send("y", o, lse_mine, lse_all.at[place.y], landed)
        lse_out[...] = lse
        found_out[...] = found
        lse_all[place.y] = lse_mine[...]

    stat_landed = countdown(y_count, lambda: engine.work(0.2, over_y))

    def grads_of(half):
        def run():
            def one(i, carry):
                d = half * y_half + i
                shares = None
                lse = lse_all[d][:blocks]
                for s in range(CORES):
                    scale = unfolded(jnp.exp(peaks[d, s][:blocks] - lse))
                    dlogit = kept[d, s] * scale - hits[d, s].astype(jnp.float32)
                    term = jnp.dot(
                        turned[pick(d, s)],
                        dlogit.astype(jnp.bfloat16),
                        preferred_element_type=jnp.float32,
                    )
                    shares = term if shares is None else shares + term
                shares = shares.astype(jnp.bfloat16).reshape(z_count, x_count, 2 * UNIT, inst)
                for axis, share in (("x", b["g_x"]), ("z", b["g_z"]), ("y", b["g_y"])):
                    for place_in, rows_in, lanes_in in spots(axis):
                        share[d, :, :, place_in] = shares[:, :, rows_in, lanes_in]
                return carry

            lax.fori_loop(0, y_half, one, 0)
            start_sums(half)

        return run

    def queue_grads():
        for half in (0, 1):
            engine.work(y_half * GRADS_COST, grads_of(half))

    def slots(name):
        return {(sign, half): b[name, sign, half] for sign in (1, -1) for half in (0, 1)}

    def part(half, count):
        return pl.ds(half * count, count)

    def put(axis, start):
        def run(value):
            stop = start + value.shape[0]
            for place_in, rows_in, lanes_in in spots(axis):
                low, high = max(place_in.start, start), min(place_in.stop, stop)
                if low < high:
                    first = rows_in.start + low - place_in.start
                    out[first : first + high - low, lanes_in] = value[low - start : high - start]

        return run

    def put_x(which):
        return put("x", which * x_part)

    x_part = SHARES["x"] * UNIT // 2

    def second_xy():
        for half in (0, 1):
            hub_sum(
                engine,
                "y",
                half,
                lambda dest, half=half: b["x_sum"].at[dest, part(half, z_half), :x_part],
                slots("xy2"),
                b["xy_sum"].at[part(half, z_half)],
                last_xy,
            )

    def second_xz(half):
        hub_sum(
            engine,
            "z",
            half,
            lambda dest: b["x_sum"].at[part(half, y_half), dest, x_part:],
            slots("xz2"),
            b["xz_sum"].at[part(half, y_half)],
            last_xz,
        )
        first_x()

    last_xy = countdown(2, lambda: direct_sum(engine, "z", put_x(0), b["xy_sum"], b["last_xy"]))
    last_xz = countdown(2, lambda: direct_sum(engine, "y", put_x(1), b["xz_sum"], b["last_xz"]))
    last_z = countdown(2, lambda: direct_sum(engine, "y", put("z", 0), b["zx_sum"], b["last_z"]))
    last_y = countdown(2, lambda: direct_sum(engine, "z", put("y", 0), b["yx_sum"], b["last_y"]))
    first_x = countdown(2, second_xy)

    def start_sums(half):
        for zh in (0, 1) if half else ():
            ring_sum(
                engine,
                "y",
                zh,
                lambda dest, zh=zh: b["g_y"].at[dest, part(zh, z_half)],
                slots("y1"),
                b["y_sum"].at[part(zh, z_half)],
                lambda zh=zh: ring_sum(
                    engine,
                    "x",
                    zh,
                    lambda dest: b["y_sum"].at[part(zh, z_half), dest],
                    slots("y2"),
                    b["yx_sum"].at[part(zh, z_half)],
                    last_y,
                ),
            )
        ring_sum(
            engine,
            "z",
            half,
            lambda dest: b["g_z"].at[part(half, y_half), dest],
            slots("z1"),
            b["z_sum"].at[part(half, y_half)],
            lambda: ring_sum(
                engine,
                "x",
                half,
                lambda dest: b["z_sum"].at[part(half, y_half), dest],
                slots("z2"),
                b["zx_sum"].at[part(half, y_half)],
                last_z,
            ),
        )
        ring_sum(
            engine,
            "x",
            half,
            lambda dest: b["g_x"].at[part(half, y_half), :, dest],
            slots("x1"),
            b["x_sum"].at[part(half, y_half)],
            lambda: second_xz(half),
        )

    c_part = inst // 32 * C_PARTS // 2
    a_from = 2 * c_part
    a_part, b_part = inst // 32 * A_PARTS // x_count, inst // 32 * B_PARTS // z_count
    b_from = a_from + a_part * x_count
    c_halves = (0, 1) if c_part else ()
    turn_a, turn_b = itertools.count(), itertools.count()
    complete = {
        o: countdown(x_count + z_count + 1 + len(c_halves), lambda o=o: engine.work(LOGITS_COST, logits_of(o)))
        for o in range(1, y_count)
    }

    complete[0] = countdown(2, lambda: engine.work(LOGITS_COST, logits_of(0)))

    def hits_next(o):
        return lambda: engine.work(HITS_COST, hits_of(o, complete[o]))

    def cut(origin, start, count):
        return f_all.at[origin, pl.ds(pl.multiple_of(start, 16), count)]

    def a_landed(o):
        origin = place.at("y", o)
        complete[o]()
        spread(
            engine,
            "x",
            next(turn_a) % 2,
            lambda: cut(origin, a_from + place.x * a_part, a_part),
            lambda p: cut(origin, a_from + p * a_part, a_part),
            lambda _: complete[o](),
        )

    def b_landed(o):
        origin = place.at("y", o)
        complete[o]()
        spread(
            engine,
            "z",
            next(turn_b) % 2,
            lambda: cut(origin, b_from + place.z * b_part, b_part),
            lambda p: cut(origin, b_from + p * b_part, b_part),
            lambda _: complete[o](),
        )

    def from_feats(start, count):
        return lambda: feats.at[pl.ds(pl.multiple_of(start, 16), count)]

    def turn_rows(base):
        def run():
            def one(i, carry):
                turned[base + i] = rows_all[base + i].T
                return carry

            lax.fori_loop(0, stored, one, 0)

        return run

    def swapped():
        complete[0]()
        engine.work(3.0, turn_rows(stored))

    start = b_from + place.z * b_part
    spread(
        engine, "y", 1, from_feats(start, b_part),
        lambda p, start=start: cut(p, start, b_part), b_landed,
    )
    start = a_from + place.x * a_part
    spread(
        engine, "y", 0, from_feats(start, a_part),
        lambda p, start=start: cut(p, start, a_part), a_landed,
    )
    engine.send("core", 1, rows, rows_all.at[pl.ds(stored, stored)], swapped)
    for o in range(1, y_count):
        engine.send("y", o, pos, p_all.at[place.y], hits_next(-o % y_count))
    for half in c_halves:
        spread(
            engine, "y", half, from_feats(half * c_part, c_part),
            lambda p, half=half: cut(p, half * c_part, c_part), lambda o: complete[o](),
        )
    for copy in locals_:
        copy.wait()
    hits_next(0)()
    engine.work(3.0, turn_rows(0))
    engine.run()


def step(sizes, info, feats, pos, rows):
    inst, width = feats.shape
    stored, size, _ = rows.shape
    buffers, copies = plan(sizes, inst, width, size, stored, pos.shape[0])
    scratch = [pltpu.VMEM(*spec) for spec in buffers.values()]
    scratch += [pltpu.SemaphoreType.DMA((n,)) for n in (3, copies, copies)]
    return pl.pallas_call(
        functools.partial(step_kernel, sizes, list(buffers)),
        out_shape=[
            jax.ShapeDtypeStruct((inst // BLK, BLK), jnp.float32),
            jax.ShapeDtypeStruct((inst // BLK, BLK), jnp.float32),
            jax.ShapeDtypeStruct((2 * UNIT, inst), jnp.float32),
        ],
        in_specs=[pl.BlockSpec(memory_space=pltpu.SMEM)] + [pl.BlockSpec(memory_space=pl.ANY)] * 3,
        out_specs=[pl.BlockSpec(memory_space=pltpu.VMEM)] * 3,
        scratch_shapes=scratch,
        compiler_params=pltpu.CompilerParams(
            collective_id=0, has_side_effects=True, vmem_limit_bytes=VMEM_LIMIT
        ),
    )(info, feats, pos, rows)


def shards(x_count, feats, weights, shortlist, slot_of, positives):
    y_count = lax.axis_size("dp") // CORES
    lab_count = lax.axis_size("label")
    sizes = (y_count, lab_count // x_count, x_count)
    dp_index, lab_index = lax.axis_index("dp"), lax.axis_index("label")
    core = dp_index % CORES
    stored, size, width = weights.shape
    inst, pos_count = positives.shape
    block_count = inst // BLK
    half_blocks = block_count // 2
    pair = jnp.stack([dp_index, dp_index + 1 - 2 * core]) * lab_count + lab_index
    slots = (pair[:, None] * stored + jnp.arange(stored, dtype=jnp.int32)).reshape(-1)
    ids = jnp.arange(slot_of.shape[0], dtype=jnp.int32)
    clusters = jnp.sum(jnp.where(slots[:, None] == slot_of[None, :], ids[None, :], 0), axis=1)
    lists = shortlist.reshape(y_count, CORES * block_count, -1)
    lists = lax.dynamic_slice_in_dim(lists, core * block_count, block_count, axis=1)
    member = jnp.any(lists[:, :, None, :] == clusters[None, None, :, None], axis=3)
    member = member.reshape(y_count, block_count, CORES, stored).astype(jnp.int32)
    chosen = jnp.sum(member[:, :half_blocks], axis=1)
    pick = jnp.sum(chosen * jnp.arange(stored, dtype=jnp.int32), axis=2)
    cluster = jnp.sum(chosen * clusters.reshape(1, CORES, stored), axis=2)
    blocks = jnp.sum(member, axis=3).transpose(0, 2, 1)
    info = jnp.concatenate([pick[..., None], cluster[..., None], blocks], axis=2)
    lse, found, grads = step(sizes, info.reshape(y_count, -1), feats, positives.T, weights)
    return (lse - found).reshape(-1), grads.astype(jnp.bfloat16).T


def solution(mesh, x_count=X_CHIPS):
    in_specs = (P("dp", None), P(("dp", "label"), None, None), P(), P(), P("dp", None))
    out_specs = (P("dp"), P("dp", "label"))
    return jax.shard_map(
        functools.partial(shards, x_count),
        mesh=mesh,
        in_specs=in_specs,
        out_specs=out_specs,
        check_vma=False,
    )
```

```python
import functools
import heapq
import itertools
import math

import jax
import jax.numpy as jnp
from jax import lax
from jax.experimental import pallas as pl
from jax.experimental.pallas import tpu as pltpu
from jax.sharding import PartitionSpec as P

BLK = 128
CORES = 2
X_CHIPS = 4
VMEM_LIMIT = 60 * 1024 * 1024
NEG_FILL = -1e30
MESH = pl.DeviceIdType.MESH
A_PARTS, B_PARTS, C_PARTS = 16, 16, 0
LINK_RATE = 51e3
LINK_DELAY = 2.5
ISSUE = 0.1
HITS_COST = 0.7
TURN_COST = 0.7
LOGITS_COST = 1.0
GRADS_COST = 0.8


class Place:
    def __init__(self, y_count, z_count, x_count):
        dp, lab = lax.axis_index("dp"), lax.axis_index("label")
        self.dp, self.lab = dp, lab
        self.y, self.core = dp // CORES, dp % CORES
        self.z, self.x = lab // x_count, lab % x_count
        self.count = {"y": y_count, "z": z_count, "x": x_count}
        self.pos = {"y": self.y, "z": self.z, "x": self.x}

    def at(self, axis, offset):
        n = self.count[axis]
        return lax.rem(self.pos[axis] + (offset % n), n)

    def device(self, axis, offset):
        if axis == "core":
            return (self.y * CORES + (1 - self.core), self.lab)
        p = self.at(axis, offset)
        if axis == "y":
            return (p * CORES + self.core, self.lab)
        if axis == "z":
            return (self.dp, p * self.count["x"] + self.x)
        return (self.dp, self.z * self.count["x"] + p)


def greet(devices):
    barrier = pltpu.get_barrier_semaphore()
    for device in devices:
        pl.semaphore_signal(barrier, inc=1, device_id=device, device_id_type=MESH)
    pl.semaphore_wait(barrier, len(devices))


class Engine:
    def __init__(self, place, send_sem, recv_sem):
        self.place, self.send_sem, self.recv_sem = place, send_sem, recv_sem
        self.ids, self.order = itertools.count(), itertools.count()
        self.sent, self.heap, self.ready = [], [], []
        self.free, self.now = {}, 0.0

    def send(self, axis, offset, src, dst, arrived):
        i = next(self.ids)
        copy = pltpu.make_async_remote_copy(
            src_ref=src,
            dst_ref=dst,
            send_sem=self.send_sem.at[i],
            recv_sem=self.recv_sem.at[i],
            device_id=self.place.device(axis, offset),
            device_id_type=MESH,
        )
        copy.start()
        self.sent.append(copy)
        hops, sign, rate = 1, 1, 6 * LINK_RATE
        if axis != "core":
            n = self.place.count[axis]
            offset = offset % n
            sign = 1 if offset <= n // 2 else -1
            hops, rate = min(offset, n - offset), LINK_RATE
        size = math.prod(src.shape) * jnp.dtype(src.dtype).itemsize
        start = max(self.now, self.free.get((axis, sign), 0.0))
        self.free[axis, sign] = start + hops * size / rate
        heapq.heappush(
            self.heap, (self.free[axis, sign] + LINK_DELAY, next(self.order), copy, arrived)
        )
        self.now += ISSUE

    def work(self, cost, run, later=False):
        heapq.heappush(self.ready, (later, next(self.order), cost, run))

    def run(self):
        while self.heap or self.ready:
            if self.ready and (not self.heap or self.heap[0][0] > self.now):
                _, _, cost, run = heapq.heappop(self.ready)
                self.now += cost
                run()
                continue
            when, _, copy, arrived = heapq.heappop(self.heap)
            self.now = max(self.now, when) + ISSUE
            copy.wait_recv()
            arrived()
        for copy in self.sent:
            copy.wait_send()


def countdown(count, run):
    left = [count]

    def one():
        left[0] -= 1
        if left[0] == 0:
            run()

    return one


def reach(n, sign, half):
    return n // 2 if (sign > 0) == (half == 0) else n // 2 - 1


def spread(engine, axis, half, source, target, arrived):
    place = engine.place
    n = place.count[axis]

    def pass_on(sign, k):
        if k < reach(n, sign, half):
            origin = place.at(axis, -sign * k)
            src = target(origin) if k else source()
            engine.send(axis, sign, src, target(origin), lambda: landed(sign, k + 1))

    def landed(sign, k):
        pass_on(sign, k)
        arrived(-sign * k % n)

    for sign in (1, -1):
        pass_on(sign, 0)


def add_into(total, term):
    def one(i, carry):
        value = total[i].astype(jnp.float32) + term[i].astype(jnp.float32)
        total[i] = value.astype(total.dtype)
        return carry

    lax.fori_loop(0, total.shape[0], one, 0)


def ring_sum(engine, axis, half, own, slots, total, done):
    place = engine.place
    n = place.count[axis]
    chains = [(sign, reach(n, sign, half)) for sign in (1, -1) if reach(n, sign, half) > 0]

    def finish():
        parts = [slots[sign, half].at[length - 1] for sign, length in chains]
        first = own(place.at(axis, 0))

        def one(i, carry):
            value = first[i].astype(jnp.float32)
            for part in parts:
                value = value + part[i].astype(jnp.float32)
            total[i] = value
            return carry

        lax.fori_loop(0, total.shape[0], one, 0)
        done()

    landed = countdown(len(chains), lambda: engine.work(0.3, finish))

    def step(sign, length, k):
        if k == length:
            landed()
            return
        ref = own(place.at(axis, sign * (length - k)))
        if k > 0:
            add_into(slots[sign, half].at[k - 1], ref)
            engine.now += 0.3
            ref = slots[sign, half].at[k - 1]
        engine.send(axis, sign, ref, slots[sign, half].at[k], lambda: step(sign, length, k + 1))

    for sign, length in chains:
        step(sign, length, 0)


def hub_sum(engine, axis, half, own, slots, total, done):
    place = engine.place
    n = place.count[axis]
    chains = [(sign, reach(n, sign, half)) for sign in (1, -1) if reach(n, sign, half) > 0]
    near, hub, third, fourth = range(4)

    def finish():
        first = own(place.at(axis, 0))
        parts = [
            slots[sign, half].at[k] for sign, length in chains for k in range(min(length, 2))
        ]

        def one(i, carry):
            value = first[i]
            for part in parts:
                value = value + part[i]
            total[i] = value
            return carry

        lax.fori_loop(0, total.shape[0], one, 0)
        done()

    landed = countdown(
        sum(min(length, 2) for _, length in chains), lambda: engine.work(0.3, finish)
    )

    def start(sign, length):
        inbox = slots[sign, half]

        def relay():
            ref = own(place.at(axis, 2 * sign))
            for k in range(fourth, hub, -1):
                if k < length:
                    add_into(inbox.at[k], ref)
                    ref = inbox.at[k]
                    engine.now += 0.2
            engine.send(axis, 2 * sign, ref, inbox.at[hub], landed)

        collected = countdown(length - 2, relay) if length > 2 else None
        for k in range(fourth, hub, -1):
            if k < length:
                engine.send(axis, (k - 1) * sign, own(place.at(axis, (k + 1) * sign)), inbox.at[k], collected)
        if length == 2:
            relay()
        engine.send(axis, sign, own(place.at(axis, sign)), inbox.at[near], landed)

    for sign, length in chains:
        start(sign, length)


def direct_sum(engine, axis, put, total, slots):
    place = engine.place
    n = place.count[axis]

    def finish():
        value = total[place.at(axis, 0)]
        for o in range(1, n):
            value = value + slots[o - 1]
        put(value)

    landed = countdown(n - 1, lambda: engine.work(0.2, finish))
    for o in range(1, n):
        engine.send(axis, o, total.at[place.at(axis, o)], slots.at[o - 1], landed)


def merge(parts, n):
    high = parts[0][0:n]
    for part in parts[1:]:
        high = jnp.maximum(high, part[0:n])
    total = sum(part[n : 2 * n] * jnp.exp(part[0:n] - high) for part in parts)
    hits = sum(part[2 * n : 3 * n] for part in parts)
    return high, total, hits


def write(ref, values):
    row = 0
    for value in values:
        ref[row : row + value.shape[0], :] = value
        row += value.shape[0]


def folded(row):
    return [row[:, i : i + BLK] for i in range(0, row.shape[1], BLK)]


def unfolded(rows):
    return jnp.concatenate([rows[i : i + 1] for i in range(rows.shape[0])], axis=1)


UNIT = 16
UNITS = [(lane, rows) for lane in range(4) for rows in range(2)]
SHARES = {"x": 3, "z": 3, "y": 2}


def units(axis):
    first = {"x": 0, "z": SHARES["x"], "y": SHARES["x"] + SHARES["z"]}[axis]
    return UNITS[first : first + SHARES[axis]]


def spots(axis):
    for i, (lane, rows) in enumerate(units(axis)):
        yield slice(i * UNIT, i * UNIT + UNIT), slice(rows * UNIT, rows * UNIT + UNIT), slice(
            lane * BLK, lane * BLK + BLK
        )


def plan(sizes, inst, width, size, stored, pos_count):
    n = dict(zip("yzx", sizes))
    y, z, x = sizes
    bf, f4 = jnp.bfloat16, jnp.float32
    tile, lse_tile = (4 * inst // BLK, BLK), (8, BLK)
    rows = {c: SHARES[c] * UNIT for c in SHARES}
    buffers = {
        "f_all": ((y, inst, width), bf),
        "p_all": ((y, pos_count, inst), jnp.int32),
        "rows_all": ((CORES * stored, size, width), bf),
        "turned": ((CORES * stored, width, size), bf),
        "kept": ((y, CORES, size, inst), f4),
        "hits": ((y, CORES, size, inst), bf),
        "peaks": ((y, CORES) + tile, f4),
        "stats": ((y,) + tile, f4),
        "lse_all": ((y,) + lse_tile, f4),
        "lse_mine": (lse_tile, f4),
        "held": ((2,) + tile, f4),
        "stat_y": ((y - 1,) + tile, f4),
        "stat_x": ((x - 1,) + tile, f4),
        "stat_z": ((z - 1,) + tile, f4),
        "g_x": ((y, z, x, rows["x"], BLK), bf),
        "g_z": ((y, z, x, rows["z"], BLK), bf),
        "g_y": ((y, z, x, rows["y"], BLK), bf),
        "x_sum": ((y, z, rows["x"], BLK), f4),
        "xy_sum": ((z, rows["x"] // 2, BLK), f4),
        "xz_sum": ((y, rows["x"] // 2, BLK), f4),
        "z_sum": ((y, x, rows["z"], BLK), f4),
        "zx_sum": ((y, rows["z"], BLK), f4),
        "y_sum": ((z, x, rows["y"], BLK), f4),
        "yx_sum": ((z, rows["y"], BLK), f4),
        "last_xy": ((z - 1, rows["x"] // 2, BLK), f4),
        "last_xz": ((y - 1, rows["x"] // 2, BLK), f4),
        "last_z": ((y - 1, rows["z"], BLK), f4),
        "last_y": ((z - 1, rows["y"], BLK), f4),
    }
    rings = {
        "x1": ("x", (y // 2, z, rows["x"], BLK), bf),
        "z1": ("z", (y // 2, x, rows["z"], BLK), bf),
        "y1": ("y", (z // 2, x, rows["y"], BLK), bf),
        "xy2": ("y", (z // 2, rows["x"] // 2, BLK), f4),
        "xz2": ("z", (y // 2, rows["x"] // 2, BLK), f4),
        "z2": ("x", (y // 2, rows["z"], BLK), f4),
        "y2": ("x", (z // 2, rows["y"], BLK), f4),
    }
    copies = 1 + 2 * (z - 1) + 2 * (y - 1)
    for name, (axis, shape, dtype) in rings.items():
        for sign in (1, -1):
            for half in (0, 1):
                steps = reach(n[axis], sign, half)
                copies += steps
                buffers[name, sign, half] = ((max(steps, 1),) + shape, dtype)
    copies += (y - 1) * (5 + (x - 1) + (z - 1)) + 2 * (y - 1) + (x - 1) + (z - 1)
    return buffers, copies


def step_kernel(sizes, names, info, feats, pos, rows, lse_out, found_out, out, *scratch):
    y_count, z_count, x_count = sizes
    place = Place(*sizes)
    b = dict(zip(names, scratch))
    local_sem, send_sem, recv_sem = scratch[len(names) :]
    inst, width = feats.shape
    stored, size, _ = rows.shape
    pos_count = pos.shape[0]
    y_half, z_half = y_count // 2, z_count // 2
    f_all, p_all, rows_all, turned = b["f_all"], b["p_all"], b["rows_all"], b["turned"]
    kept, hits, peaks, stats, lse_all, lse_mine, held = (
        b[k] for k in ("kept", "hits", "peaks", "stats", "lse_all", "lse_mine", "held")
    )
    blocks = inst // BLK
    locals_ = [
        pltpu.make_async_copy(rows, rows_all.at[pl.ds(0, stored)], local_sem.at[0]),
        pltpu.make_async_copy(feats, f_all.at[place.y], local_sem.at[1]),
        pltpu.make_async_copy(pos, p_all.at[place.y], local_sem.at[2]),
    ]
    for copy in locals_:
        copy.start()
    greet(
        [
            place.device(axis, offset)
            for axis, n in (("y", y_count), ("x", x_count), ("z", z_count))
            for offset in range(1, n)
        ]
        + [place.device("core", 1)]
    )
    engine = Engine(place, send_sem, recv_sem)
    fields = 2 + blocks

    def pick(d, s):
        return s * stored + info[d, s * fields]

    def hits_of(offset, done):
        def run():
            d = place.at("y", offset)

            def one(s, carry):
                shape = (size, inst)
                label = info[d, s * fields + 1] * size + lax.broadcasted_iota(jnp.int32, shape, 0)
                hit = p_all[d, 0:1, :] == label
                for p in range(1, pos_count):
                    hit = hit | (p_all[d, p : p + 1, :] == label)
                hits[d, s] = jnp.where(hit, 1.0 / pos_count, 0.0).astype(jnp.bfloat16)
                return carry

            lax.fori_loop(0, CORES, one, 0)
            done()

        return run

    def logits_of(offset):
        def run():
            d = place.at("y", offset)

            def one(s, carry):
                logits = lax.dot_general(
                    rows_all[pick(d, s)],
                    f_all[d],
                    (((1,), (1,)), ((), ())),
                    preferred_element_type=jnp.float32,
                )
                member = jnp.concatenate(
                    [jnp.full((1, BLK), info[d, s * fields + 2 + i]) for i in range(blocks)], axis=1
                )
                valid = jnp.where(member > 0, logits, NEG_FILL)
                high = jnp.max(valid, axis=0, keepdims=True)
                power = jnp.exp(valid - high)
                kept[d, s] = power
                total = jnp.sum(power, axis=0, keepdims=True)
                found = jnp.sum(hits[d, s].astype(jnp.float32) * logits, axis=0, keepdims=True)
                write(peaks.at[d, s], folded(high) + folded(total) + folded(found))
                return carry

            lax.fori_loop(0, CORES, one, 0)
            stats[d] = jnp.zeros_like(stats[d])
            write(stats.at[d], merge([peaks[d, s] for s in range(CORES)], blocks))
            if offset % y_count:
                engine.send("y", offset, stats.at[d], b["stat_y"].at[offset - 1], stat_landed)
            else:
                stat_landed()

        return run

    def turn_rows(i):
        def run():
            turned[i] = rows_all[i].T

        return run

    def over_y():
        for i in range(CORES * stored):
            engine.work(TURN_COST, turn_rows(i), later=True)
        held[0] = jnp.zeros_like(held[0])
        write(
            held.at[0],
            merge([stats[place.y]] + [b["stat_y"][o] for o in range(y_count - 1)], blocks),
        )
        landed = countdown(x_count - 1, lambda: engine.work(0.2, over_x))
        for o in range(1, x_count):
            engine.send("x", o, held.at[0], b["stat_x"].at[o - 1], landed)

    def over_x():
        held[1] = jnp.zeros_like(held[1])
        write(held.at[1], merge([held[0]] + [b["stat_x"][o] for o in range(x_count - 1)], blocks))
        landed = countdown(z_count - 1, lambda: engine.work(0.2, over_z))
        for o in range(1, z_count):
            engine.send("z", o, held.at[1], b["stat_z"].at[o - 1], landed)

    def over_z():
        high, total, found = merge([held[1]] + [b["stat_z"][o] for o in range(z_count - 1)], blocks)
        lse = high + jnp.log(total)
        lse_mine[...] = jnp.zeros_like(lse_mine)
        write(lse_mine, [lse])
        landed = countdown(y_count - 1, queue_grads)
        for o in range(1, y_count):
            engine.send("y", o, lse_mine, lse_all.at[place.y], landed)
        lse_out[...] = lse
        found_out[...] = found
        lse_all[place.y] = lse_mine[...]

    stat_landed = countdown(y_count, lambda: engine.work(0.2, over_y))

    def grads_of(half):
        def run():
            def one(i, carry):
                d = half * y_half + i
                shares = None
                lse = lse_all[d][:blocks]
                for s in range(CORES):
                    scale = unfolded(jnp.exp(peaks[d, s][:blocks] - lse))
                    dlogit = kept[d, s] * scale - hits[d, s].astype(jnp.float32)
                    term = jnp.dot(
                        turned[pick(d, s)],
                        dlogit.astype(jnp.bfloat16),
                        preferred_element_type=jnp.float32,
                    )
                    shares = term if shares is None else shares + term
                shares = shares.astype(jnp.bfloat16).reshape(z_count, x_count, 2 * UNIT, inst)
                for axis, share in (("x", b["g_x"]), ("z", b["g_z"]), ("y", b["g_y"])):
                    for place_in, rows_in, lanes_in in spots(axis):
                        share[d, :, :, place_in] = shares[:, :, rows_in, lanes_in]
                return carry

            lax.fori_loop(0, y_half, one, 0)
            start_sums(half)

        return run

    def queue_grads():
        for half in (0, 1):
            engine.work(y_half * GRADS_COST, grads_of(half), later=True)

    def slots(name):
        return {(sign, half): b[name, sign, half] for sign in (1, -1) for half in (0, 1)}

    def part(half, count):
        return pl.ds(half * count, count)

    def put(axis, start):
        def run(value):
            stop = start + value.shape[0]
            for place_in, rows_in, lanes_in in spots(axis):
                low, high = max(place_in.start, start), min(place_in.stop, stop)
                if low < high:
                    first = rows_in.start + low - place_in.start
                    out[first : first + high - low, lanes_in] = value[low - start : high - start]

        return run

    def put_x(which):
        return put("x", which * x_part)

    x_part = SHARES["x"] * UNIT // 2

    def second_xy():
        for half in (0, 1):
            hub_sum(
                engine,
                "y",
                half,
                lambda dest, half=half: b["x_sum"].at[dest, part(half, z_half), :x_part],
                slots("xy2"),
                b["xy_sum"].at[part(half, z_half)],
                last_xy,
            )

    def second_xz(half):
        hub_sum(
            engine,
            "z",
            half,
            lambda dest: b["x_sum"].at[part(half, y_half), dest, x_part:],
            slots("xz2"),
            b["xz_sum"].at[part(half, y_half)],
            last_xz,
        )
        first_x()

    last_xy = countdown(2, lambda: direct_sum(engine, "z", put_x(0), b["xy_sum"], b["last_xy"]))
    last_xz = countdown(2, lambda: direct_sum(engine, "y", put_x(1), b["xz_sum"], b["last_xz"]))
    last_z = countdown(2, lambda: direct_sum(engine, "y", put("z", 0), b["zx_sum"], b["last_z"]))
    last_y = countdown(2, lambda: direct_sum(engine, "z", put("y", 0), b["yx_sum"], b["last_y"]))
    first_x = countdown(2, second_xy)

    def start_sums(half):
        for zh in (0, 1) if half else ():
            ring_sum(
                engine,
                "y",
                zh,
                lambda dest, zh=zh: b["g_y"].at[dest, part(zh, z_half)],
                slots("y1"),
                b["y_sum"].at[part(zh, z_half)],
                lambda zh=zh: ring_sum(
                    engine,
                    "x",
                    zh,
                    lambda dest: b["y_sum"].at[part(zh, z_half), dest],
                    slots("y2"),
                    b["yx_sum"].at[part(zh, z_half)],
                    last_y,
                ),
            )
        ring_sum(
            engine,
            "z",
            half,
            lambda dest: b["g_z"].at[part(half, y_half), dest],
            slots("z1"),
            b["z_sum"].at[part(half, y_half)],
            lambda: ring_sum(
                engine,
                "x",
                half,
                lambda dest: b["z_sum"].at[part(half, y_half), dest],
                slots("z2"),
                b["zx_sum"].at[part(half, y_half)],
                last_z,
            ),
        )
        ring_sum(
            engine,
            "x",
            half,
            lambda dest: b["g_x"].at[part(half, y_half), :, dest],
            slots("x1"),
            b["x_sum"].at[part(half, y_half)],
            lambda: second_xz(half),
        )

    c_part = inst // 32 * C_PARTS // 2
    a_from = 2 * c_part
    a_part, b_part = inst // 32 * A_PARTS // x_count, inst // 32 * B_PARTS // z_count
    b_from = a_from + a_part * x_count
    c_halves = (0, 1) if c_part else ()
    turn_a, turn_b = itertools.count(), itertools.count()
    complete = {
        o: countdown(x_count + z_count + 1 + len(c_halves), lambda o=o: engine.work(LOGITS_COST, logits_of(o)))
        for o in range(1, y_count)
    }

    complete[0] = countdown(2, lambda: engine.work(LOGITS_COST, logits_of(0)))

    def hits_next(o):
        return lambda: engine.work(HITS_COST, hits_of(o, complete[o]))

    def cut(origin, start, count):
        return f_all.at[origin, pl.ds(pl.multiple_of(start, 16), count)]

    def a_landed(o):
        origin = place.at("y", o)
        complete[o]()
        spread(
            engine,
            "x",
            next(turn_a) % 2,
            lambda: cut(origin, a_from + place.x * a_part, a_part),
            lambda p: cut(origin, a_from + p * a_part, a_part),
            lambda _: complete[o](),
        )

    def b_landed(o):
        origin = place.at("y", o)
        complete[o]()
        spread(
            engine,
            "z",
            next(turn_b) % 2,
            lambda: cut(origin, b_from + place.z * b_part, b_part),
            lambda p: cut(origin, b_from + p * b_part, b_part),
            lambda _: complete[o](),
        )

    def from_feats(start, count):
        return lambda: feats.at[pl.ds(pl.multiple_of(start, 16), count)]

    def swapped():
        complete[0]()

    start = b_from + place.z * b_part
    spread(
        engine, "y", 1, from_feats(start, b_part),
        lambda p, start=start: cut(p, start, b_part), b_landed,
    )
    start = a_from + place.x * a_part
    spread(
        engine, "y", 0, from_feats(start, a_part),
        lambda p, start=start: cut(p, start, a_part), a_landed,
    )
    engine.send("core", 1, rows, rows_all.at[pl.ds(stored, stored)], swapped)
    for o in range(1, y_count):
        engine.send("y", o, pos, p_all.at[place.y], hits_next(-o % y_count))
    for half in c_halves:
        spread(
            engine, "y", half, from_feats(half * c_part, c_part),
            lambda p, half=half: cut(p, half * c_part, c_part), lambda o: complete[o](),
        )
    for copy in locals_:
        copy.wait()
    hits_next(0)()
    engine.run()


def step(sizes, info, feats, pos, rows):
    inst, width = feats.shape
    stored, size, _ = rows.shape
    buffers, copies = plan(sizes, inst, width, size, stored, pos.shape[0])
    scratch = [pltpu.VMEM(*spec) for spec in buffers.values()]
    scratch += [pltpu.SemaphoreType.DMA((n,)) for n in (3, copies, copies)]
    return pl.pallas_call(
        functools.partial(step_kernel, sizes, list(buffers)),
        out_shape=[
            jax.ShapeDtypeStruct((inst // BLK, BLK), jnp.float32),
            jax.ShapeDtypeStruct((inst // BLK, BLK), jnp.float32),
            jax.ShapeDtypeStruct((2 * UNIT, inst), jnp.float32),
        ],
        in_specs=[pl.BlockSpec(memory_space=pltpu.SMEM)] + [pl.BlockSpec(memory_space=pl.ANY)] * 3,
        out_specs=[pl.BlockSpec(memory_space=pltpu.VMEM)] * 3,
        scratch_shapes=scratch,
        compiler_params=pltpu.CompilerParams(
            collective_id=0, has_side_effects=True, vmem_limit_bytes=VMEM_LIMIT
        ),
    )(info, feats, pos, rows)


def shards(x_count, feats, weights, shortlist, slot_of, positives):
    y_count = lax.axis_size("dp") // CORES
    lab_count = lax.axis_size("label")
    sizes = (y_count, lab_count // x_count, x_count)
    dp_index, lab_index = lax.axis_index("dp"), lax.axis_index("label")
    core = dp_index % CORES
    stored, size, width = weights.shape
    inst, pos_count = positives.shape
    block_count = inst // BLK
    half_blocks = block_count // 2
    pair = jnp.stack([dp_index, dp_index + 1 - 2 * core]) * lab_count + lab_index
    slots = (pair[:, None] * stored + jnp.arange(stored, dtype=jnp.int32)).reshape(-1)
    ids = jnp.arange(slot_of.shape[0], dtype=jnp.int32)
    clusters = jnp.sum(jnp.where(slots[:, None] == slot_of[None, :], ids[None, :], 0), axis=1)
    lists = shortlist.reshape(y_count, CORES * block_count, -1)
    lists = lax.dynamic_slice_in_dim(lists, core * block_count, block_count, axis=1)
    member = jnp.any(lists[:, :, None, :] == clusters[None, None, :, None], axis=3)
    member = member.reshape(y_count, block_count, CORES, stored).astype(jnp.int32)
    chosen = jnp.sum(member[:, :half_blocks], axis=1)
    pick = jnp.sum(chosen * jnp.arange(stored, dtype=jnp.int32), axis=2)
    cluster = jnp.sum(chosen * clusters.reshape(1, CORES, stored), axis=2)
    blocks = jnp.sum(member, axis=3).transpose(0, 2, 1)
    info = jnp.concatenate([pick[..., None], cluster[..., None], blocks], axis=2)
    lse, found, grads = step(sizes, info.reshape(y_count, -1), feats, positives.T, weights)
    return (lse - found).reshape(-1), grads.astype(jnp.bfloat16).T


def solution(mesh, x_count=X_CHIPS):
    in_specs = (P("dp", None), P(("dp", "label"), None, None), P(), P(), P("dp", None))
    out_specs = (P("dp"), P("dp", "label"))
    return jax.shard_map(
        functools.partial(shards, x_count),
        mesh=mesh,
        in_specs=in_specs,
        out_specs=out_specs,
        check_vma=False,
    )
```

```python
import functools
import heapq
import itertools
import math

import jax
import jax.numpy as jnp
from jax import lax
from jax.experimental import pallas as pl
from jax.experimental.pallas import tpu as pltpu
from jax.sharding import PartitionSpec as P

BLK = 128
CORES = 2
X_CHIPS = 4
VMEM_LIMIT = 60 * 1024 * 1024
NEG_FILL = -1e30
MESH = pl.DeviceIdType.MESH
A_PARTS, B_PARTS, C_PARTS = 16, 16, 0
LINK_RATE = 51e3
LINK_DELAY = 2.5
ISSUE = 0.04
HITS_COST = 0.35
TURN_COST = 0.7
LOGITS_COST = 0.5
GRADS_COST = 0.8


class Place:
    def __init__(self, y_count, z_count, x_count):
        dp, lab = lax.axis_index("dp"), lax.axis_index("label")
        self.dp, self.lab = dp, lab
        self.y, self.core = dp // CORES, dp % CORES
        self.z, self.x = lab // x_count, lab % x_count
        self.count = {"y": y_count, "z": z_count, "x": x_count}
        self.pos = {"y": self.y, "z": self.z, "x": self.x}

    def at(self, axis, offset):
        n = self.count[axis]
        return lax.rem(self.pos[axis] + (offset % n), n)

    def device(self, axis, offset):
        if axis == "core":
            return (self.y * CORES + (1 - self.core), self.lab)
        p = self.at(axis, offset)
        if axis == "y":
            return (p * CORES + self.core, self.lab)
        if axis == "z":
            return (self.dp, p * self.count["x"] + self.x)
        return (self.dp, self.z * self.count["x"] + p)


def greet(devices):
    barrier = pltpu.get_barrier_semaphore()
    for device in devices:
        pl.semaphore_signal(barrier, inc=1, device_id=device, device_id_type=MESH)
    pl.semaphore_wait(barrier, len(devices))


class Engine:
    def __init__(self, place, send_sem, recv_sem):
        self.place, self.send_sem, self.recv_sem = place, send_sem, recv_sem
        self.ids, self.order = itertools.count(), itertools.count()
        self.sent, self.heap, self.ready = [], [], []
        self.free, self.now = {}, 0.0

    def send(self, axis, offset, src, dst, arrived):
        i = next(self.ids)
        copy = pltpu.make_async_remote_copy(
            src_ref=src,
            dst_ref=dst,
            send_sem=self.send_sem.at[i],
            recv_sem=self.recv_sem.at[i],
            device_id=self.place.device(axis, offset),
            device_id_type=MESH,
        )
        copy.start()
        self.sent.append(copy)
        hops, sign, rate = 1, 1, 6 * LINK_RATE
        if axis != "core":
            n = self.place.count[axis]
            offset = offset % n
            sign = 1 if offset <= n // 2 else -1
            hops, rate = min(offset, n - offset), LINK_RATE
        size = math.prod(src.shape) * jnp.dtype(src.dtype).itemsize
        start = max(self.now, self.free.get((axis, sign), 0.0))
        self.free[axis, sign] = start + hops * size / rate
        heapq.heappush(
            self.heap, (self.free[axis, sign] + LINK_DELAY, next(self.order), copy, arrived)
        )
        self.now += ISSUE

    def work(self, cost, run, later=False):
        heapq.heappush(self.ready, (later, next(self.order), cost, run))

    def run(self):
        while self.heap or self.ready:
            if self.ready and (not self.heap or self.heap[0][0] > self.now):
                _, _, cost, run = heapq.heappop(self.ready)
                self.now += cost
                run()
                continue
            when, _, copy, arrived = heapq.heappop(self.heap)
            self.now = max(self.now, when) + ISSUE
            copy.wait_recv()
            arrived()
        for copy in self.sent:
            copy.wait_send()


def countdown(count, run):
    left = [count]

    def one():
        left[0] -= 1
        if left[0] == 0:
            run()

    return one


def reach(n, sign, half):
    return n // 2 if (sign > 0) == (half == 0) else n // 2 - 1


def spread(engine, axis, half, source, target, arrived):
    place = engine.place
    n = place.count[axis]

    def pass_on(sign, k):
        if k < reach(n, sign, half):
            origin = place.at(axis, -sign * k)
            src = target(origin) if k else source()
            engine.send(axis, sign, src, target(origin), lambda: landed(sign, k + 1))

    def landed(sign, k):
        pass_on(sign, k)
        arrived(-sign * k % n)

    for sign in (1, -1):
        pass_on(sign, 0)


def add_into(total, term):
    def one(i, carry):
        value = total[i].astype(jnp.float32) + term[i].astype(jnp.float32)
        total[i] = value.astype(total.dtype)
        return carry

    lax.fori_loop(0, total.shape[0], one, 0)


def ring_sum(engine, axis, half, own, slots, total, done):
    place = engine.place
    n = place.count[axis]
    chains = [(sign, reach(n, sign, half)) for sign in (1, -1) if reach(n, sign, half) > 0]

    def finish():
        parts = [slots[sign, half].at[length - 1] for sign, length in chains]
        first = own(place.at(axis, 0))

        def one(i, carry):
            value = first[i].astype(jnp.float32)
            for part in parts:
                value = value + part[i].astype(jnp.float32)
            total[i] = value
            return carry

        lax.fori_loop(0, total.shape[0], one, 0)
        done()

    landed = countdown(len(chains), lambda: engine.work(0.3, finish))

    def step(sign, length, k):
        if k == length:
            landed()
            return
        ref = own(place.at(axis, sign * (length - k)))
        if k > 0:
            add_into(slots[sign, half].at[k - 1], ref)
            engine.now += 0.3
            ref = slots[sign, half].at[k - 1]
        engine.send(axis, sign, ref, slots[sign, half].at[k], lambda: step(sign, length, k + 1))

    for sign, length in chains:
        step(sign, length, 0)


def hub_sum(engine, axis, half, own, slots, total, done):
    place = engine.place
    n = place.count[axis]
    chains = [(sign, reach(n, sign, half)) for sign in (1, -1) if reach(n, sign, half) > 0]
    near, hub, third, fourth = range(4)

    def finish():
        first = own(place.at(axis, 0))
        parts = [
            slots[sign, half].at[k] for sign, length in chains for k in range(min(length, 2))
        ]

        def one(i, carry):
            value = first[i]
            for part in parts:
                value = value + part[i]
            total[i] = value
            return carry

        lax.fori_loop(0, total.shape[0], one, 0)
        done()

    landed = countdown(
        sum(min(length, 2) for _, length in chains), lambda: engine.work(0.3, finish)
    )

    def start(sign, length):
        inbox = slots[sign, half]

        def relay():
            ref = own(place.at(axis, 2 * sign))
            for k in range(fourth, hub, -1):
                if k < length:
                    add_into(inbox.at[k], ref)
                    ref = inbox.at[k]
                    engine.now += 0.2
            engine.send(axis, 2 * sign, ref, inbox.at[hub], landed)

        collected = countdown(length - 2, relay) if length > 2 else None
        for k in range(fourth, hub, -1):
            if k < length:
                engine.send(axis, (k - 1) * sign, own(place.at(axis, (k + 1) * sign)), inbox.at[k], collected)
        if length == 2:
            relay()
        engine.send(axis, sign, own(place.at(axis, sign)), inbox.at[near], landed)

    for sign, length in chains:
        start(sign, length)


def direct_sum(engine, axis, put, total, slots):
    place = engine.place
    n = place.count[axis]

    def finish():
        value = total[place.at(axis, 0)]
        for o in range(1, n):
            value = value + slots[o - 1]
        put(value)

    landed = countdown(n - 1, lambda: engine.work(0.2, finish))
    for o in range(1, n):
        engine.send(axis, o, total.at[place.at(axis, o)], slots.at[o - 1], landed)


def merge(parts, n):
    high = parts[0][0:n]
    for part in parts[1:]:
        high = jnp.maximum(high, part[0:n])
    total = sum(part[n : 2 * n] * jnp.exp(part[0:n] - high) for part in parts)
    hits = sum(part[2 * n : 3 * n] for part in parts)
    return high, total, hits


def write(ref, values):
    row = 0
    for value in values:
        ref[row : row + value.shape[0], :] = value
        row += value.shape[0]


def folded(row):
    return [row[:, i : i + BLK] for i in range(0, row.shape[1], BLK)]


def unfolded(rows):
    return jnp.concatenate([rows[i : i + 1] for i in range(rows.shape[0])], axis=1)


UNIT = 16
UNITS = [(lane, rows) for lane in range(4) for rows in range(2)]
SHARES = {"x": 3, "z": 3, "y": 2}


def units(axis):
    first = {"x": 0, "z": SHARES["x"], "y": SHARES["x"] + SHARES["z"]}[axis]
    return UNITS[first : first + SHARES[axis]]


def spots(axis):
    for i, (lane, rows) in enumerate(units(axis)):
        yield slice(i * UNIT, i * UNIT + UNIT), slice(rows * UNIT, rows * UNIT + UNIT), slice(
            lane * BLK, lane * BLK + BLK
        )


def plan(sizes, inst, width, size, stored, pos_count):
    n = dict(zip("yzx", sizes))
    y, z, x = sizes
    bf, f4 = jnp.bfloat16, jnp.float32
    tile, lse_tile = (4 * inst // BLK, BLK), (8, BLK)
    rows = {c: SHARES[c] * UNIT for c in SHARES}
    buffers = {
        "f_all": ((y, inst, width), bf),
        "p_all": ((y, pos_count, inst), jnp.int32),
        "rows_all": ((CORES * stored, size, width), bf),
        "turned": ((CORES * stored, width, size), bf),
        "kept": ((y, CORES, size, inst), f4),
        "hits": ((y, CORES, size, inst), bf),
        "peaks": ((y, CORES) + tile, f4),
        "stats": ((y,) + tile, f4),
        "lse_all": ((y,) + lse_tile, f4),
        "lse_mine": (lse_tile, f4),
        "held": ((2,) + tile, f4),
        "stat_y": ((y - 1,) + tile, f4),
        "stat_x": ((x - 1,) + tile, f4),
        "stat_z": ((z - 1,) + tile, f4),
        "g_x": ((y, z, x, rows["x"], BLK), bf),
        "g_z": ((y, z, x, rows["z"], BLK), bf),
        "g_y": ((y, z, x, rows["y"], BLK), bf),
        "x_sum": ((y, z, rows["x"], BLK), f4),
        "xy_sum": ((z, rows["x"] // 2, BLK), f4),
        "xz_sum": ((y, rows["x"] // 2, BLK), f4),
        "z_sum": ((y, x, rows["z"], BLK), f4),
        "zx_sum": ((y, rows["z"], BLK), f4),
        "y_sum": ((z, x, rows["y"], BLK), f4),
        "yx_sum": ((z, rows["y"], BLK), f4),
        "last_xy": ((z - 1, rows["x"] // 2, BLK), f4),
        "last_xz": ((y - 1, rows["x"] // 2, BLK), f4),
        "last_z": ((y - 1, rows["z"], BLK), f4),
        "last_y": ((z - 1, rows["y"], BLK), f4),
    }
    rings = {
        "x1": ("x", (y // 2, z, rows["x"], BLK), bf),
        "z1": ("z", (y // 2, x, rows["z"], BLK), bf),
        "y1": ("y", (z // 2, x, rows["y"], BLK), bf),
        "xy2": ("y", (z // 2, rows["x"] // 2, BLK), f4),
        "xz2": ("z", (y // 2, rows["x"] // 2, BLK), f4),
        "z2": ("x", (y // 2, rows["z"], BLK), f4),
        "y2": ("x", (z // 2, rows["y"], BLK), f4),
    }
    copies = 1 + 2 * (z - 1) + 2 * (y - 1)
    for name, (axis, shape, dtype) in rings.items():
        for sign in (1, -1):
            for half in (0, 1):
                steps = reach(n[axis], sign, half)
                copies += steps
                buffers[name, sign, half] = ((max(steps, 1),) + shape, dtype)
    copies += (y - 1) * (5 + (x - 1) + (z - 1)) + 2 * (y - 1) + (x - 1) + (z - 1)
    return buffers, copies


def step_kernel(sizes, names, info, feats, pos, rows, lse_out, found_out, out, *scratch):
    y_count, z_count, x_count = sizes
    place = Place(*sizes)
    b = dict(zip(names, scratch))
    local_sem, send_sem, recv_sem = scratch[len(names) :]
    inst, width = feats.shape
    stored, size, _ = rows.shape
    pos_count = pos.shape[0]
    y_half, z_half = y_count // 2, z_count // 2
    f_all, p_all, rows_all, turned = b["f_all"], b["p_all"], b["rows_all"], b["turned"]
    kept, hits, peaks, stats, lse_all, lse_mine, held = (
        b[k] for k in ("kept", "hits", "peaks", "stats", "lse_all", "lse_mine", "held")
    )
    blocks = inst // BLK
    locals_ = [
        pltpu.make_async_copy(rows, rows_all.at[pl.ds(0, stored)], local_sem.at[0]),
        pltpu.make_async_copy(feats, f_all.at[place.y], local_sem.at[1]),
        pltpu.make_async_copy(pos, p_all.at[place.y], local_sem.at[2]),
    ]
    for copy in locals_:
        copy.start()
    greet(
        [
            place.device(axis, offset)
            for axis, n in (("y", y_count), ("x", x_count), ("z", z_count))
            for offset in range(1, n)
        ]
        + [place.device("core", 1)]
    )
    engine = Engine(place, send_sem, recv_sem)
    fields = 2 + blocks

    def pick(d, s):
        return s * stored + info[d, s * fields]

    def hits_of(offset, s, done):
        def run():
            d = place.at("y", offset)

            shape = (size, inst)
            label = info[d, s * fields + 1] * size + lax.broadcasted_iota(jnp.int32, shape, 0)
            hit = p_all[d, 0:1, :] == label
            for p in range(1, pos_count):
                hit = hit | (p_all[d, p : p + 1, :] == label)
            hits[d, s] = jnp.where(hit, 1.0 / pos_count, 0.0).astype(jnp.bfloat16)
            done()

        return run

    def logits_of(offset, s, done):
        def run():
            d = place.at("y", offset)

            logits = lax.dot_general(
                rows_all[pick(d, s)],
                f_all[d],
                (((1,), (1,)), ((), ())),
                preferred_element_type=jnp.float32,
            )
            member = jnp.concatenate(
                [jnp.full((1, BLK), info[d, s * fields + 2 + i]) for i in range(blocks)], axis=1
            )
            valid = jnp.where(member > 0, logits, NEG_FILL)
            high = jnp.max(valid, axis=0, keepdims=True)
            power = jnp.exp(valid - high)
            kept[d, s] = power
            total = jnp.sum(power, axis=0, keepdims=True)
            found = jnp.sum(hits[d, s].astype(jnp.float32) * logits, axis=0, keepdims=True)
            write(peaks.at[d, s], folded(high) + folded(total) + folded(found))
            done()

        return run

    def stats_of(offset):
        def run():
            d = place.at("y", offset)
            stats[d] = jnp.zeros_like(stats[d])
            write(stats.at[d], merge([peaks[d, s] for s in range(CORES)], blocks))
            if offset % y_count:
                engine.send("y", offset, stats.at[d], b["stat_y"].at[offset - 1], stat_landed)
            else:
                stat_landed()

        return run

    def turn_rows(i):
        def run():
            turned[i] = rows_all[i].T

        return run

    def over_y():
        for i in range(CORES * stored):
            engine.work(TURN_COST, turn_rows(i), later=True)
        held[0] = jnp.zeros_like(held[0])
        write(
            held.at[0],
            merge([stats[place.y]] + [b["stat_y"][o] for o in range(y_count - 1)], blocks),
        )
        landed = countdown(x_count - 1, lambda: engine.work(0.2, over_x))
        for o in range(1, x_count):
            engine.send("x", o, held.at[0], b["stat_x"].at[o - 1], landed)

    def over_x():
        held[1] = jnp.zeros_like(held[1])
        write(held.at[1], merge([held[0]] + [b["stat_x"][o] for o in range(x_count - 1)], blocks))
        landed = countdown(z_count - 1, lambda: engine.work(0.2, over_z))
        for o in range(1, z_count):
            engine.send("z", o, held.at[1], b["stat_z"].at[o - 1], landed)

    def over_z():
        high, total, found = merge([held[1]] + [b["stat_z"][o] for o in range(z_count - 1)], blocks)
        lse = high + jnp.log(total)
        lse_mine[...] = jnp.zeros_like(lse_mine)
        write(lse_mine, [lse])
        landed = countdown(y_count - 1, queue_grads)
        for o in range(1, y_count):
            engine.send("y", o, lse_mine, lse_all.at[place.y], landed)
        lse_out[...] = lse
        found_out[...] = found
        lse_all[place.y] = lse_mine[...]

    stat_landed = countdown(y_count, lambda: engine.work(0.2, over_y))

    def grads_of(half):
        def run():
            def one(i, carry):
                d = half * y_half + i
                shares = None
                lse = lse_all[d][:blocks]
                for s in range(CORES):
                    scale = unfolded(jnp.exp(peaks[d, s][:blocks] - lse))
                    dlogit = kept[d, s] * scale - hits[d, s].astype(jnp.float32)
                    term = jnp.dot(
                        turned[pick(d, s)],
                        dlogit.astype(jnp.bfloat16),
                        preferred_element_type=jnp.float32,
                    )
                    shares = term if shares is None else shares + term
                shares = shares.astype(jnp.bfloat16).reshape(z_count, x_count, 2 * UNIT, inst)
                for axis, share in (("x", b["g_x"]), ("z", b["g_z"]), ("y", b["g_y"])):
                    for place_in, rows_in, lanes_in in spots(axis):
                        share[d, :, :, place_in] = shares[:, :, rows_in, lanes_in]
                return carry

            lax.fori_loop(0, y_half, one, 0)
            start_sums(half)

        return run

    def queue_grads():
        for half in (0, 1):
            engine.work(y_half * GRADS_COST, grads_of(half), later=True)

    def slots(name):
        return {(sign, half): b[name, sign, half] for sign in (1, -1) for half in (0, 1)}

    def part(half, count):
        return pl.ds(half * count, count)

    def put(axis, start):
        def run(value):
            stop = start + value.shape[0]
            for place_in, rows_in, lanes_in in spots(axis):
                low, high = max(place_in.start, start), min(place_in.stop, stop)
                if low < high:
                    first = rows_in.start + low - place_in.start
                    out[first : first + high - low, lanes_in] = value[low - start : high - start]

        return run

    def put_x(which):
        return put("x", which * x_part)

    x_part = SHARES["x"] * UNIT // 2

    def second_xy():
        for half in (0, 1):
            hub_sum(
                engine,
                "y",
                half,
                lambda dest, half=half: b["x_sum"].at[dest, part(half, z_half), :x_part],
                slots("xy2"),
                b["xy_sum"].at[part(half, z_half)],
                last_xy,
            )

    def second_xz(half):
        hub_sum(
            engine,
            "z",
            half,
            lambda dest: b["x_sum"].at[part(half, y_half), dest, x_part:],
            slots("xz2"),
            b["xz_sum"].at[part(half, y_half)],
            last_xz,
        )
        first_x()

    last_xy = countdown(2, lambda: direct_sum(engine, "z", put_x(0), b["xy_sum"], b["last_xy"]))
    last_xz = countdown(2, lambda: direct_sum(engine, "y", put_x(1), b["xz_sum"], b["last_xz"]))
    last_z = countdown(2, lambda: direct_sum(engine, "y", put("z", 0), b["zx_sum"], b["last_z"]))
    last_y = countdown(2, lambda: direct_sum(engine, "z", put("y", 0), b["yx_sum"], b["last_y"]))
    first_x = countdown(2, second_xy)

    def start_sums(half):
        for zh in (0, 1) if half else ():
            ring_sum(
                engine,
                "y",
                zh,
                lambda dest, zh=zh: b["g_y"].at[dest, part(zh, z_half)],
                slots("y1"),
                b["y_sum"].at[part(zh, z_half)],
                lambda zh=zh: ring_sum(
                    engine,
                    "x",
                    zh,
                    lambda dest: b["y_sum"].at[part(zh, z_half), dest],
                    slots("y2"),
                    b["yx_sum"].at[part(zh, z_half)],
                    last_y,
                ),
            )
        ring_sum(
            engine,
            "z",
            half,
            lambda dest: b["g_z"].at[part(half, y_half), dest],
            slots("z1"),
            b["z_sum"].at[part(half, y_half)],
            lambda: ring_sum(
                engine,
                "x",
                half,
                lambda dest: b["z_sum"].at[part(half, y_half), dest],
                slots("z2"),
                b["zx_sum"].at[part(half, y_half)],
                last_z,
            ),
        )
        ring_sum(
            engine,
            "x",
            half,
            lambda dest: b["g_x"].at[part(half, y_half), :, dest],
            slots("x1"),
            b["x_sum"].at[part(half, y_half)],
            lambda: second_xz(half),
        )

    c_part = inst // 32 * C_PARTS // 2
    a_from = 2 * c_part
    a_part, b_part = inst // 32 * A_PARTS // x_count, inst // 32 * B_PARTS // z_count
    b_from = a_from + a_part * x_count
    c_halves = (0, 1) if c_part else ()
    def queue_logits(o):
        landed = countdown(CORES, stats_of(o))
        for s in range(CORES):
            engine.work(LOGITS_COST, logits_of(o, s, landed))

    turn_a, turn_b = itertools.count(), itertools.count()
    complete = {
        o: countdown(x_count + z_count + CORES + len(c_halves), lambda o=o: queue_logits(o))
        for o in range(1, y_count)
    }

    complete[0] = countdown(1 + CORES, lambda: queue_logits(0))

    def hits_next(o):
        def run():
            for s in range(CORES):
                engine.work(HITS_COST, hits_of(o, s, complete[o]))

        return run

    def cut(origin, start, count):
        return f_all.at[origin, pl.ds(pl.multiple_of(start, 16), count)]

    def a_landed(o):
        origin = place.at("y", o)
        complete[o]()
        spread(
            engine,
            "x",
            next(turn_a) % 2,
            lambda: cut(origin, a_from + place.x * a_part, a_part),
            lambda p: cut(origin, a_from + p * a_part, a_part),
            lambda _: complete[o](),
        )

    def b_landed(o):
        origin = place.at("y", o)
        complete[o]()
        spread(
            engine,
            "z",
            next(turn_b) % 2,
            lambda: cut(origin, b_from + place.z * b_part, b_part),
            lambda p: cut(origin, b_from + p * b_part, b_part),
            lambda _: complete[o](),
        )

    def from_feats(start, count):
        return lambda: feats.at[pl.ds(pl.multiple_of(start, 16), count)]

    def swapped():
        complete[0]()

    start = b_from + place.z * b_part
    spread(
        engine, "y", 1, from_feats(start, b_part),
        lambda p, start=start: cut(p, start, b_part), b_landed,
    )
    start = a_from + place.x * a_part
    spread(
        engine, "y", 0, from_feats(start, a_part),
        lambda p, start=start: cut(p, start, a_part), a_landed,
    )
    engine.send("core", 1, rows, rows_all.at[pl.ds(stored, stored)], swapped)
    for o in range(1, y_count):
        engine.send("y", o, pos, p_all.at[place.y], hits_next(-o % y_count))
    for half in c_halves:
        spread(
            engine, "y", half, from_feats(half * c_part, c_part),
            lambda p, half=half: cut(p, half * c_part, c_part), lambda o: complete[o](),
        )
    for copy in locals_:
        copy.wait()
    hits_next(0)()
    engine.run()


def step(sizes, info, feats, pos, rows):
    inst, width = feats.shape
    stored, size, _ = rows.shape
    buffers, copies = plan(sizes, inst, width, size, stored, pos.shape[0])
    scratch = [pltpu.VMEM(*spec) for spec in buffers.values()]
    scratch += [pltpu.SemaphoreType.DMA((n,)) for n in (3, copies, copies)]
    return pl.pallas_call(
        functools.partial(step_kernel, sizes, list(buffers)),
        out_shape=[
            jax.ShapeDtypeStruct((inst // BLK, BLK), jnp.float32),
            jax.ShapeDtypeStruct((inst // BLK, BLK), jnp.float32),
            jax.ShapeDtypeStruct((2 * UNIT, inst), jnp.float32),
        ],
        in_specs=[pl.BlockSpec(memory_space=pltpu.SMEM)] + [pl.BlockSpec(memory_space=pl.ANY)] * 3,
        out_specs=[pl.BlockSpec(memory_space=pltpu.VMEM)] * 3,
        scratch_shapes=scratch,
        compiler_params=pltpu.CompilerParams(
            collective_id=0, has_side_effects=True, vmem_limit_bytes=VMEM_LIMIT
        ),
    )(info, feats, pos, rows)


def shards(x_count, feats, weights, shortlist, slot_of, positives):
    y_count = lax.axis_size("dp") // CORES
    lab_count = lax.axis_size("label")
    sizes = (y_count, lab_count // x_count, x_count)
    dp_index, lab_index = lax.axis_index("dp"), lax.axis_index("label")
    core = dp_index % CORES
    stored, size, width = weights.shape
    inst, pos_count = positives.shape
    block_count = inst // BLK
    half_blocks = block_count // 2
    pair = jnp.stack([dp_index, dp_index + 1 - 2 * core]) * lab_count + lab_index
    slots = (pair[:, None] * stored + jnp.arange(stored, dtype=jnp.int32)).reshape(-1)
    ids = jnp.arange(slot_of.shape[0], dtype=jnp.int32)
    clusters = jnp.sum(jnp.where(slots[:, None] == slot_of[None, :], ids[None, :], 0), axis=1)
    lists = shortlist.reshape(y_count, CORES * block_count, -1)
    lists = lax.dynamic_slice_in_dim(lists, core * block_count, block_count, axis=1)
    member = jnp.any(lists[:, :, None, :] == clusters[None, None, :, None], axis=3)
    member = member.reshape(y_count, block_count, CORES, stored).astype(jnp.int32)
    chosen = jnp.sum(member[:, :half_blocks], axis=1)
    pick = jnp.sum(chosen * jnp.arange(stored, dtype=jnp.int32), axis=2)
    cluster = jnp.sum(chosen * clusters.reshape(1, CORES, stored), axis=2)
    blocks = jnp.sum(member, axis=3).transpose(0, 2, 1)
    info = jnp.concatenate([pick[..., None], cluster[..., None], blocks], axis=2)
    lse, found, grads = step(sizes, info.reshape(y_count, -1), feats, positives.T, weights)
    return (lse - found).reshape(-1), grads.astype(jnp.bfloat16).T


def solution(mesh, x_count=X_CHIPS):
    in_specs = (P("dp", None), P(("dp", "label"), None, None), P(), P(), P("dp", None))
    out_specs = (P("dp"), P("dp", "label"))
    return jax.shard_map(
        functools.partial(shards, x_count),
        mesh=mesh,
        in_specs=in_specs,
        out_specs=out_specs,
        check_vma=False,
    )
```
